128 devices in a mesh: dom: 128 (over y, x, z, core).
Axes of the slice: x: 4, y: 4, z: 4, core: 2. Of those that a mesh axis runs over, the one named last changes fastest.
Arguments:
- disp: float32 [3, 524288], P(None, 'dom'), may hold values from -6 to 6
- direction: float32 [3, 524288], P(None, 'dom'), may hold values from -6 to 6
- load: float32 [3, 524288], P(None, 'dom'), may hold values from -6 to 6
- blocks: bfloat16 [96, 96, 65536], P(None, None, 'dom'), may hold values from -0.625 to 0.625
- elem_nodes: int32 [32, 65536], P(None, 'dom'), may hold values from 0 to 5119
- halo_send: int32 [512, 256], P('dom'), may hold values from 0 to 4095
- master_nodes: int32 [16384, 12], P('dom'), may hold values from 0 to 4095
- slave_nodes: int32 [16384, 12], P('dom'), may hold values from 0 to 4095
- mortar_send: int32 [128, 128, 32], P('dom'), may hold values from 0 to 127
- mortar_count: int32 [128, 128], P('dom'), may hold values from 0 to 32, as said below
- pair_slave: int32 [524288], P('dom'), may hold values from 0 to 127
- slave_mortar: float32 [9, 36, 524288], P(None, None, 'dom'), may hold values from -1.2 to 1.2
- master_mortar: float32 [9, 36, 524288], P(None, None, 'dom'), may hold values from -1.2 to 1.2
- gap_offset: float32 [9, 524288], P(None, 'dom'), may hold values from -6 to 6
Outputs:
- residual: float32 [3, 524288], P(None, 'dom')
- applied: float32 [3, 524288], P(None, 'dom')
The draws below stay inside these ranges and needn't reach their ends.
Inputs may be any that keep to these rules, and one draw needn't show every extreme that they name: `mortar_count`: at most 32 live slots from one partition to one peer; every partition fills all 32 slots to at least one peer.
All inputs are finite; a program needn't handle non-finite values.
Results may differ from the reference program's by a relative error of at most 0.0012.
Values may be sent and summed in bfloat16 or wider, within the bound.
No kernel may reach another device: no remote copies, remote signals or barrier semaphores. Data moves between devices by JAX's collectives and lax.ppermute only.
A program may use at most 128 MiB of HBM per device.

```python
import jax
import jax.numpy as jnp
from jax import lax

E_DEV = 512
MS = 32
REACH = 2
QUAD = 9
NODE_DEV = 4096
HS = 256
NB = 4
SEGS = 128
NODES = 524288
ELEMS = 65536
PAIRS = 524288
N_DOM = 128


def draw_mortar_count(key, part):
    key = jax.random.fold_in(key, 11)
    first, second, third = jax.random.split(key, 3)
    weight = jax.random.randint(first, (N_DOM, 1), 1, 5)
    base = jax.random.randint(second, (N_DOM, N_DOM), 0, MS + 1)
    counted = jnp.minimum(MS, base * weight // 2)
    fullest = jax.random.randint(third, (N_DOM,), 0, N_DOM)
    counted = jnp.where(jnp.arange(N_DOM)[None, :] == fullest[:, None], MS, counted)
    return counted.astype(jnp.int32)


def set_ends(drawn, rng, low, top_value):
    dims = drawn.shape
    index_at = [jax.random.randint(jax.random.fold_in(rng, axis), (), 0, dims[axis]) for axis in range(len(dims))]
    drawn = drawn.at[tuple(index_at)].set(low)
    longest = dims.index(max(dims))
    index_at[longest] = (index_at[longest] + 1) % dims[longest]
    return drawn.at[tuple(index_at)].set(top_value)


def block_scale(stream_key, shape, shards, least, high):
    def one(position, blocks):
        steps = jax.random.uniform(jax.random.fold_in(jax.random.fold_in(stream_key, 6), position), (blocks,), jnp.float32, least / len(shards), high / len(shards))
        return jnp.repeat(jnp.exp(steps), shape[position] // blocks).reshape((-1,) + (1,) * (len(shape) - position - 1))

    level = one(*shards[0])
    for cut in shards[1:]:
        level = level * one(*cut)
    return level


def gaussian(own_key, dims, scale, reach, pieces=(), kind=jnp.bfloat16):
    loudness = block_scale(own_key, dims, pieces, -0.22, 0.18) if pieces else 1.0
    values = jax.random.normal(own_key, dims, jnp.float32) * scale * loudness
    return jnp.minimum(jnp.maximum(values, -reach), reach).astype(kind)


def setup_inputs(seed: int = 0) -> dict:
    keys = jax.random.split(jax.random.key(seed), 15)
    return {
        "disp": gaussian(keys[0], (3, NODES), 1.0, 6.0, ((1, 128),), jnp.float32),
        "direction": gaussian(keys[1], (3, NODES), 1.0, 6.0, ((1, 128),), jnp.float32),
        "load": gaussian(keys[2], (3, NODES), 1.0, 6.0, ((1, 128),), jnp.float32),
        "blocks": gaussian(keys[3], (96, 96, ELEMS), 96 ** -0.5, 0.625, ((2, 128),)),
        "elem_nodes": set_ends(jax.random.randint(keys[4], (32, ELEMS), 0, NODE_DEV + NB * HS), jax.random.fold_in(keys[4], 1), 0, (NODE_DEV + NB * HS) - 1).astype(jnp.int32),
        "halo_send": set_ends(jax.random.randint(keys[5], (N_DOM * NB, HS), 0, NODE_DEV), jax.random.fold_in(keys[5], 1), 0, NODE_DEV - 1).astype(jnp.int32),
        "master_nodes": set_ends(jax.random.randint(keys[6], (N_DOM * SEGS, 12), 0, NODE_DEV), jax.random.fold_in(keys[6], 1), 0, NODE_DEV - 1).astype(jnp.int32),
        "slave_nodes": set_ends(jax.random.randint(keys[7], (N_DOM * SEGS, 12), 0, NODE_DEV), jax.random.fold_in(keys[7], 1), 0, NODE_DEV - 1).astype(jnp.int32),
        "mortar_send": set_ends(jax.random.randint(keys[8], (N_DOM, N_DOM, MS), 0, SEGS), jax.random.fold_in(keys[8], 1), 0, SEGS - 1).astype(jnp.int32),
        "mortar_count": draw_mortar_count(jax.random.fold_in(keys[14], 71), 0),
        "pair_slave": set_ends(jax.random.randint(keys[10], (PAIRS,), 0, SEGS), jax.random.fold_in(keys[10], 1), 0, SEGS - 1).astype(jnp.int32),
        "slave_mortar": gaussian(keys[11], (QUAD, 36, PAIRS), 0.2, 1.2, ((2, 128),), jnp.float32),
        "master_mortar": gaussian(keys[12], (QUAD, 36, PAIRS), 0.2, 1.2, ((2, 128),), jnp.float32),
        "gap_offset": gaussian(keys[13], (QUAD, PAIRS), 1.0, 6.0, ((1, 128),), jnp.float32),
    }


def offsets():
    return [move for move in range(-REACH, REACH + 1) if move != 0]


def apply_block(matrix, vector):
    return jnp.einsum("qkp,kp->qp", matrix, vector, precision=lax.Precision.HIGHEST)


def adjoint_block(matrix, vector):
    return jnp.einsum("qkp,qp->kp", matrix, vector, precision=lax.Precision.HIGHEST)


def device_work(extended, fields, blocks, elem_nodes, slave_nodes, pair_slave, slave_mortar, master_mortar, gap_offset, remote, live):
    elements = blocks.shape[2]
    picked = extended[:, elem_nodes].reshape(2, 96, elements)
    forces = jnp.einsum("ije,wje->wie", blocks.astype(jnp.float32), picked.astype(jnp.float32), precision=lax.Precision.HIGHEST)
    forces = forces.reshape(6, 32, elements)
    totals = jnp.zeros((6, extended.shape[1]), jnp.float32).at[:, elem_nodes].add(forces)
    slave_index = slave_nodes[pair_slave]
    nearby = fields[:, slave_index].transpose(0, 2, 1).reshape(72, -1)
    opening = apply_block(slave_mortar, nearby[:36]) + apply_block(master_mortar, remote[:36]) + gap_offset
    tangent = apply_block(slave_mortar, nearby[36:]) + apply_block(master_mortar, remote[36:])
    pressure = jax.nn.softplus(opening) * live
    increment = jax.nn.sigmoid(opening) * tangent * live
    slave_force = jnp.concatenate([adjoint_block(slave_mortar, pressure), adjoint_block(slave_mortar, increment)], 0)
    master_force = jnp.concatenate([adjoint_block(master_mortar, pressure), adjoint_block(master_mortar, increment)], 0)
    totals = totals.at[:, slave_index.T].add(slave_force.reshape(6, 12, -1))
    return totals, master_force


def reference(disp, direction, load, blocks, elem_nodes, halo_send, master_nodes, slave_nodes, mortar_send, mortar_count, pair_slave, slave_mortar, master_mortar, gap_offset):
    parts = N_DOM
    moves = offsets()
    fields = jnp.concatenate([disp, direction], 0).reshape(6, parts, NODE_DEV)
    coarse = fields.astype(jnp.bfloat16)
    send_lists = halo_send.reshape(parts, NB, HS)
    outgoing = jax.vmap(lambda field, rows: field[:, rows], in_axes=(1, 0), out_axes=1)(coarse, send_lists)
    arrived = jnp.stack([jnp.roll(outgoing[:, :, slot], moves[slot], axis=1) for slot in range(NB)], axis=2)
    extended = jnp.concatenate([coarse, arrived.reshape(6, parts, NB * HS)], axis=2)
    master_table = master_nodes.reshape(parts, SEGS, 12)
    master_index = jax.vmap(lambda table, segs: table[segs])(master_table, mortar_send)
    master_values = jax.vmap(lambda field, index: field[:, index], in_axes=(1, 0))(fields, master_index)
    master_values = master_values.transpose(0, 1, 4, 2, 3).reshape(parts, 72, parts, MS)
    live_slots = (jnp.arange(MS, dtype=jnp.int32)[None, None, :] < mortar_count[:, :, None]).astype(jnp.float32)
    remote = master_values.transpose(2, 1, 0, 3).reshape(parts, 72, parts * MS)
    live = live_slots.transpose(1, 0, 2).reshape(parts, 1, parts * MS)
    pairs_dev = parts * MS
    inputs = (extended.transpose(1, 0, 2), fields.transpose(1, 0, 2), blocks.reshape(96, 96, parts, E_DEV).transpose(2, 0, 1, 3), elem_nodes.reshape(32, parts, E_DEV).transpose(1, 0, 2), slave_nodes.reshape(parts, SEGS, 12), pair_slave.reshape(parts, pairs_dev), slave_mortar.reshape(QUAD, 36, parts, pairs_dev).transpose(2, 0, 1, 3), master_mortar.reshape(QUAD, 36, parts, pairs_dev).transpose(2, 0, 1, 3), gap_offset.reshape(QUAD, parts, pairs_dev).transpose(1, 0, 2), remote, live)
    totals, master_force = lax.map(lambda items: device_work(*items), inputs)
    returned_force = master_force.reshape(parts, 72, parts, MS).transpose(2, 1, 0, 3)
    sums = totals[:, :, NODE_DEV:].reshape(parts, 6, NB, HS)
    owned = totals[:, :, :NODE_DEV]

    def finish(own, rows, index, back, shared):
        for slot in range(NB):
            own = own.at[:, rows[slot]].add(shared[slot])
        return own.at[:, index.transpose(2, 0, 1)].add(back.reshape(6, 12, parts, MS))

    shared_back = jnp.stack([jnp.roll(sums[:, :, slot], -moves[slot], axis=0) for slot in range(NB)], axis=1)
    owned = jax.vmap(finish)(owned, send_lists, master_index, returned_force, shared_back)
    owned = owned.transpose(1, 0, 2).reshape(6, parts * NODE_DEV)
    return load - owned[:3], owned[3:]
```

```python
import jax
import jax.numpy as jnp
from jax import lax
from jax.experimental import pallas as pl
from jax.experimental.pallas import tpu as pltpu
from jax.sharding import PartitionSpec as P

REACH = 2
F32, BF16, I32 = jnp.float32, jnp.bfloat16, jnp.int32
LANES = 128
WIDE = 256
WORDS = 10
QUADS = 9
FACE = 12
LIMIT = 32767.0
VMEM_BYTES = 56 * 1024 * 1024


def offsets():
    return [move for move in range(-REACH, REACH + 1) if move != 0]


def shifted(value, axis, steps):
    count = lax.axis_size(axis)
    pairs = [(source, (source + steps) % count) for source in range(count)]
    return lax.ppermute(value, axis, pairs)


def indicator(row, count):
    number = lax.broadcasted_iota(I32, (count, row.shape[1]), 0)
    return jnp.where(number == row, 1.0, 0.0).astype(BF16)


def cut(value):
    high = value.astype(BF16)
    return high, (value - high.astype(F32)).astype(BF16)


def choose(wide, group, groups):
    total = jnp.where(group == 0, wide[0:8], 0.0)
    for g in range(1, groups):
        total = total + jnp.where(group == g, wide[8 * g : 8 * g + 8], 0.0)
    return total


def gather(parts, row, groups):
    hits = indicator(row & (WIDE - 1), WIDE)
    wide = jnp.dot(parts[0], hits, preferred_element_type=F32)
    for part in parts[1:]:
        wide = wide + jnp.dot(part, hits, preferred_element_type=F32)
    return choose(wide, row >> 8, groups)


def scatter(value, row, groups):
    high = value.astype(BF16).astype(F32)
    low = value - high
    group = row >> 8
    wide = []
    for g in range(groups):
        here = group == g
        wide += [jnp.where(here, high, 0.0), jnp.where(here, low, 0.0)]
    wide = jnp.concatenate(wide, 0).astype(BF16)
    hits = indicator(row & (WIDE - 1), WIDE)
    return across(wide, hits)


def across(left, right):
    return lax.dot_general(left, right, (((1,), (1,)), ((), ())), preferred_element_type=F32)


def fill_table(table, disp, direction):
    table[...] = jnp.zeros(table.shape, F32)
    for g in range(disp.shape[1] // WIDE):
        table[8 * g : 8 * g + 3, :] = disp[:, WIDE * g : WIDE * g + WIDE]
        table[8 * g + 3 : 8 * g + 6, :] = direction[:, WIDE * g : WIDE * g + WIDE]


def turn(v):
    lane = lax.broadcasted_iota(I32, v[0].shape, 1)
    low = lane < 64
    even = (lane & 32) == 0
    a0 = jnp.where(low, v[0], pltpu.roll(v[2], 64, 1))
    a2 = jnp.where(low, pltpu.roll(v[0], 64, 1), v[2])
    a1 = jnp.where(low, v[1], pltpu.roll(v[3], 64, 1))
    a3 = jnp.where(low, pltpu.roll(v[1], 64, 1), v[3])
    return [
        jnp.where(even, a0, pltpu.roll(a1, 32, 1)),
        jnp.where(even, pltpu.roll(a0, 96, 1), a1),
        jnp.where(even, a2, pltpu.roll(a3, 32, 1)),
        jnp.where(even, pltpu.roll(a2, 96, 1), a3),
    ]


def put_words(out, base, tails, words):
    for b, block in enumerate(turn([words[8 * q : 8 * q + 8] for q in range(4)])):
        out[pl.ds(base + WORDS * b, 8), :] = block
    tails[...] = words[32:40]


def put_tails(out, tails, count):
    for h in range(2):
        rows = turn([tails[pl.ds(4 * h + q, count, stride=8), :] for q in range(4)])
        for b in range(4):
            out[pl.ds(WORDS * b + 8 + h, count, stride=4 * WORDS), :] = rows[b]


def get_tails(source, tails, count):
    for h in range(2):
        rows = turn(
            [source[pl.ds(WORDS * b + 8 + h, count, stride=4 * WORDS), :] for b in range(4)]
        )
        for q in range(4):
            tails[pl.ds(4 * h + q, count, stride=8), :] = rows[q]


def get_words(source, base, tail):
    blocks = turn([source[pl.ds(base + WORDS * b, 8), :] for b in range(4)])
    return jnp.concatenate(blocks + [tail], 0)


def step_of(level):
    return jnp.exp(level.astype(F32) * (0.25 * 0.6931471805599453))


def level_of(values):
    top = jnp.max(jnp.abs(values), axis=0, keepdims=True)
    return jnp.ceil(jnp.log(jnp.maximum(top, 1e-30)) * (4.0 / 0.6931471805599453))


def split_words(words):
    second = (words << 16) >> 16
    first = (words - second) >> 16
    return first, second


def decode(words):
    out = []
    row = lax.broadcasted_iota(I32, (8, LANES), 0)
    halves = split_words(words)
    for half in halves:
        scale = step_of(half[36:37]) * (1.0 / LIMIT)
        value = half.astype(F32) * scale
        out.append(jnp.concatenate([value[:32], jnp.where(row < 4, value[32:40], 0.0)], 0))
    return out[0], out[1], halves[0][37:38].astype(F32)


def encode(values):
    level = level_of(values)
    code = jnp.round(values * (LIMIT / step_of(level)))
    row = lax.broadcasted_iota(I32, values.shape, 0)
    return jnp.where(row == 36, level, code)


def fold2(a, b, distance):
    row = lax.broadcasted_iota(I32, a.shape, 0)
    first = (row & distance) == 0
    return jnp.where(first, a, b) + pltpu.roll(jnp.where(first, b, a), 8 - distance, 0)


def fold(v):
    v = [fold2(v[2 * r], v[2 * r + 1], 1) for r in range(4)]
    v = [fold2(v[2 * r], v[2 * r + 1], 2) for r in range(2)]
    return fold2(v[0], v[1], 4)


def tail_rows(block):
    return jnp.concatenate([block, jnp.zeros((4, LANES), F32)], 0)


def contract(mortar, lane, first, second):
    sums = ([], [])
    for q in range(QUADS):
        pieces = [mortar[q, 8 * t : 8 * t + 8, lane : lane + LANES] for t in range(4)]
        pieces.append(tail_rows(mortar[q, 32:36, lane : lane + LANES]))
        for field, out in zip((first, second), sums):
            total = pieces[0] * field[0:8]
            for t in range(1, 5):
                total = total + pieces[t] * field[8 * t : 8 * t + 8]
            out.append(total)
    last = fold2(sums[0][8], sums[1][8], 1)
    last = last + pltpu.roll(last, 6, 0)
    last = last + pltpu.roll(last, 4, 0)
    return fold(sums[0][:8]), fold(sums[1][:8]), last


def adjoint(mortar, lane, weights):
    rows = [(weights[q : q + 1], weights[8 + q : 9 + q]) for q in range(8)]
    rows.append((weights[16:17], weights[17:18]))
    sums = []
    for t in range(5):
        pair = [None, None]
        for q in range(QUADS):
            if t < 4:
                piece = mortar[q, 8 * t : 8 * t + 8, lane : lane + LANES]
            else:
                piece = tail_rows(mortar[q, 32:36, lane : lane + LANES])
            for w in range(2):
                term = piece * rows[q][w]
                pair[w] = term if q == 0 else pair[w] + term
        sums.append(pair)
    return [jnp.concatenate([pair[w] for pair in sums], 0) for w in range(2)]


def fill_faces(faces, parts, nodes):
    for a in range(FACE):
        faces[pl.ds(a, 8, stride=FACE), :] = gather(parts, nodes[a : a + 1, :], 16)


def padded_fields(faces):
    pad = jnp.zeros((4, LANES), F32)
    return jnp.concatenate([faces[0:36], pad], 0), jnp.concatenate([faces[36:72], pad], 0)


def pack_kernel(disp, direction, halo, nodes, send, count, s0, s1, s2, s3, out, slots, table, faces, square, tails):
    fill_table(table, disp, direction)
    parts = cut(table[...])
    for o, piece in enumerate((s0, s1, s2, s3)):
        piece[...] = gather(parts[:1], halo[o : o + 1, :], 16)
    fill_faces(faces, parts, nodes)
    first, second = padded_fields(faces)
    row = lax.broadcasted_iota(I32, first.shape, 0)
    codes = [encode(first), encode(second)]
    codes[0] = jnp.where(row == 37, 1.0, codes[0])
    left = []
    for code in codes:
        high = jnp.floor(code * (1.0 / 256.0))
        left += [high, code - 256.0 * high]
    left = jnp.concatenate(left, 0).astype(BF16)
    square[...] = jnp.zeros(square.shape, I32)
    square[0:32, :] = send[...]
    square[32:33, :] = count[...]
    turned = square[...].T
    lane = lax.broadcasted_iota(I32, turned.shape, 1)
    square[...] = jnp.where(lane < turned[:, 32:33], turned, -1)
    lane = lax.broadcasted_iota(I32, (32, LANES), 1)
    rows = square[pl.ds(0, 32, stride=4), :]
    for b in range(1, 4):
        moved = pltpu.roll(square[pl.ds(b, 32, stride=4), :], 32 * b, 1)
        rows = jnp.where((lane >> 5) == b, moved, rows)
    slots[...] = rows

    def group_pair(i, carry):
        hits = [indicator(slots[pl.ds(2 * i + t, 1), :], LANES) for t in range(2)]
        wide = jnp.dot(left, jnp.concatenate(hits, 1), preferred_element_type=F32)
        for t in range(2):
            here = wide[:, LANES * t : LANES * t + LANES]
            first = (here[0:40] * 256.0 + here[40:80]).astype(I32)
            second = (here[80:120] * 256.0 + here[120:160]).astype(I32)
            base = pl.multiple_of(80 * i, 8) + 40 * t
            at = pl.multiple_of(16 * i, 8) + 8 * t
            put_words(out, base, tails.at[pl.ds(at, 8), :], (first << 16) + second)
        return carry

    lax.fori_loop(0, 16, group_pair, 0)
    put_tails(out, tails, 32)


def element_kernel(disp, direction, p0, p1, p2, p3, nodes, blocks, own, s0, s1, s2, s3, table, hits, x, y, held, sums, sems):
    chunk = blocks.shape[0] // sems.shape[0]
    copies = [
        pltpu.make_async_copy(
            blocks.at[pl.ds(chunk * n, chunk)], held.at[pl.ds(chunk * n, chunk)], sems.at[n]
        )
        for n in range(sems.shape[0])
    ]
    for copy in copies:
        copy.start()
    fill_table(table, disp, direction)
    for o, piece in enumerate((p0, p1, p2, p3)):
        table[8 * (16 + o) : 8 * (17 + o), :] = piece[...]
    coarse = table[...].astype(BF16)
    elements = nodes.shape[1]

    def gather_node(a, carry):
        for h in range(elements // WIDE):
            row = nodes[pl.ds(a, 1), WIDE * h : WIDE * h + WIDE]
            hit = indicator(row & (WIDE - 1), WIDE)
            at = pl.multiple_of(a * elements, WIDE) + WIDE * h
            hits[:, pl.ds(at, WIDE)] = hit
            wide = jnp.dot(coarse, hit, preferred_element_type=F32)
            picked = choose(wide, row >> 8, 20)
            for part in range(WIDE // LANES):
                x[2 * h + part, pl.ds(a, 8, stride=32), :] = picked[
                    :, LANES * part : LANES * part + LANES
                ]
        return carry

    lax.fori_loop(0, 32, gather_node, 0)
    y[...] = jnp.zeros(y.shape, F32)
    for n, copy in enumerate(copies):
        copy.wait()
        for part in range(elements // LANES):

            def eight_rows(i, carry, part=part, n=n):
                u, v = [], []
                for r in range(8):
                    block = held[
                        chunk * n + 8 * i + r, :, LANES * part : LANES * part + LANES
                    ].astype(F32)
                    for w, out in enumerate((u, v)):
                        total = block[0:8] * x[part, 96 * w : 96 * w + 8, :]
                        for t in range(1, 12):
                            total = total + block[8 * t : 8 * t + 8] * x[
                                part, 96 * w + 8 * t : 96 * w + 8 * t + 8, :
                            ]
                        out.append(total)
                at = pl.multiple_of(chunk * n + 8 * i, 8)
                y[part, pl.ds(at, 8), :] = fold(u)
                y[part, pl.ds(96 + at, 8), :] = fold(v)
                return carry

            lax.fori_loop(0, chunk // 8, eight_rows, 0)
    sums[...] = jnp.zeros(sums.shape, F32)

    def scatter_node(a, carry):
        for h in range(elements // WIDE):
            row = nodes[pl.ds(a, 1), WIDE * h : WIDE * h + WIDE] >> 8
            value = jnp.concatenate(
                [y[2 * h + part, pl.ds(a, 8, stride=32), :] for part in range(2)], 1
            )
            high = value.astype(BF16).astype(F32)
            low = value - high
            wide = []
            for g in range(20):
                here = row == g
                wide += [jnp.where(here, high, 0.0), jnp.where(here, low, 0.0)]
            wide = jnp.concatenate(wide, 0).astype(BF16)
            at = pl.multiple_of(a * elements, WIDE) + WIDE * h
            sums[...] += across(wide, hits[:, pl.ds(at, WIDE)])
        return carry

    lax.fori_loop(0, 32, scatter_node, 0)
    for g in range(16):
        own[8 * g : 8 * g + 8, :] = sums[16 * g : 16 * g + 8, :] + sums[16 * g + 8 : 16 * g + 16, :]
    for o, piece in enumerate((s0, s1, s2, s3)):
        g = 16 + o
        piece[...] = sums[16 * g : 16 * g + 8, :] + sums[16 * g + 8 : 16 * g + 16, :]


def near_kernel(disp, direction, nodes, pair, mortar, gap, out, table, faces, left):
    step = pl.program_id(0)

    @pl.when(step == 0)
    def _():
        fill_table(table, disp, direction)
        fill_faces(faces, cut(table[...]), nodes)
        first, second = padded_fields(faces)
        parts = cut(jnp.concatenate([first, second], 0))
        left[...] = jnp.concatenate(parts, 0)

    groups = out.shape[1] // LANES
    rows = [pair[pl.ds(step * groups + t, 1), :] for t in range(groups)]
    hits = jnp.concatenate([indicator(row, LANES) for row in rows], 1)
    wide = jnp.dot(left[...], hits, preferred_element_type=F32)
    wide = wide[:80] + wide[80:]
    number = lax.broadcasted_iota(I32, (8, LANES), 0)
    for t in range(groups):
        lane = LANES * t
        field = wide[:, lane : lane + LANES]
        opening, tangent, last = contract(mortar, lane, field[:40], field[40:])
        out[0:8, lane : lane + LANES] = opening + gap[0:8, lane : lane + LANES]
        out[8:16, lane : lane + LANES] = tangent
        extra = jnp.where((number & 1) == 0, gap[8:9, lane : lane + LANES], 0.0)
        out[16:24, lane : lane + LANES] = last + extra


def react(opening, tangent, live):
    fade = jnp.exp(-jnp.abs(opening))
    pressure = jnp.maximum(opening, 0.0) + jnp.log1p(fade)
    share = jnp.where(opening >= 0.0, 1.0, fade) / (1.0 + fade)
    return pressure * live, share * tangent * live


def far_kernel(arrived, near, mortar, out, weights, tails, back):
    groups = near.shape[1] // LANES
    get_tails(arrived, tails, groups)
    number = lax.broadcasted_iota(I32, (8, LANES), 0)
    for t in range(groups):
        lane = LANES * t
        words = get_words(arrived, 40 * t, tails[8 * t : 8 * t + 8, :])
        first, second, live = decode(words)
        opening, tangent, last = contract(mortar, lane, first, second)
        opening = opening + near[0:8, lane : lane + LANES]
        tangent = tangent + near[8:16, lane : lane + LANES]
        last = last + near[16:24, lane : lane + LANES]
        pressure, increment = react(opening, tangent, live)
        ninth = react(last[0:1], last[1:2], live)
        ninth = jnp.where((number & 1) == 0, ninth[0], ninth[1])
        here = jnp.concatenate([pressure, increment, ninth], 0)
        weights[:, lane : lane + LANES] = here
        first, second = (encode(force).astype(I32) for force in adjoint(mortar, lane, here))
        put_words(out, 40 * t, back.at[8 * t : 8 * t + 8, :], (first << 16) + second)
    put_tails(out, back, groups)


def add_faces(faces, nodes):
    total = None
    for a in range(FACE):
        term = scatter(faces[pl.ds(a, 8, stride=FACE), :], nodes[a : a + 1, :], 16)
        total = term if a == 0 else total + term
    return total


def merge(total, groups):
    return [total[16 * g : 16 * g + 8] + total[16 * g + 8 : 16 * g + 16] for g in range(groups)]


def slave_kernel(own, p0, p1, p2, p3, halo, nodes, pair, mortar, weights, out, sums, faces):
    step = pl.program_id(0)

    @pl.when(step == 0)
    def _():
        sums[...] = jnp.zeros(sums.shape, F32)

    groups = weights.shape[1] // LANES
    rows = [pair[pl.ds(step * groups + t, 1), :] for t in range(groups)]
    hits = jnp.concatenate([indicator(row, LANES) for row in rows], 1)
    forces = []
    for t in range(groups):
        lane = LANES * t
        force = jnp.concatenate(adjoint(mortar, lane, weights[:, lane : lane + LANES]), 0)
        forces.append(jnp.concatenate(cut(force), 0))
    sums[...] += across(jnp.concatenate(forces, 1), hits)

    @pl.when(step == pl.num_programs(0) - 1)
    def _():
        faces[...] = jnp.zeros(faces.shape, F32)
        faces[0:36, :] = sums[0:36, :] + sums[80:116, :]
        faces[36:72, :] = sums[40:76, :] + sums[120:156, :]
        total = add_faces(faces, nodes)
        for o, piece in enumerate((p0, p1, p2, p3)):
            total = total + scatter(piece[...], halo[o : o + 1, :], 16)
        for g, rows in enumerate(merge(total, 16)):
            out[8 * g : 8 * g + 8, :] = own[8 * g : 8 * g + 8, :] + rows


def last_kernel(arrived, slots, nodes, base, load, residual, applied, tails, forces, hits, faces):
    get_tails(arrived, tails, 32)

    def group(i, carry):
        at = pl.multiple_of(8 * i, 8)
        words = get_words(arrived, pl.multiple_of(40 * i, 8), tails[pl.ds(at, 8), :])
        first, second, _ = decode(words)
        force = jnp.concatenate([first, second], 0)
        lane = pl.multiple_of(LANES * i, LANES)
        forces[:, pl.ds(lane, LANES)] = jnp.concatenate(cut(force), 0)
        hits[:, pl.ds(lane, LANES)] = indicator(slots[pl.ds(i, 1), :], LANES)
        return carry

    lax.fori_loop(0, 32, group, 0)
    sums = across(forces[...], hits[...])
    faces[...] = jnp.zeros(faces.shape, F32)
    faces[0:36, :] = sums[0:36] + sums[80:116]
    faces[36:72, :] = sums[40:76] + sums[120:156]
    for g, rows in enumerate(merge(add_faces(faces, nodes), 16)):
        rows = rows + base[8 * g : 8 * g + 8, :]
        at = WIDE * g
        residual[:, at : at + WIDE] = load[:, at : at + WIDE] - rows[0:3]
        applied[:, at : at + WIDE] = rows[3:6]


def shape(dims, kind=F32):
    return jax.ShapeDtypeStruct(dims, kind)


def whole(dims):
    return pl.BlockSpec(dims, lambda *_: (0,) * len(dims))


def call(kernel, results, scratch, flops, size, **extra):
    return pl.pallas_call(
        kernel,
        out_shape=results,
        scratch_shapes=scratch,
        compiler_params=pltpu.CompilerParams(vmem_limit_bytes=VMEM_BYTES),
        cost_estimate=pl.CostEstimate(flops=flops, bytes_accessed=size, transcendentals=0),
        **extra,
    )


def on_device(
    disp,
    direction,
    load,
    blocks,
    elem_nodes,
    halo_send,
    master_nodes,
    slave_nodes,
    mortar_send,
    mortar_count,
    pair_slave,
    slave_mortar,
    master_mortar,
    gap_offset,
):
    peers = lax.axis_size("dom")
    moves = offsets()
    elements = elem_nodes.shape[1]
    pairs = pair_slave.shape[0]
    groups = pairs // LANES
    masters, slaves = master_nodes.T, slave_nodes.T
    send = mortar_send[0].T
    pair = pair_slave.reshape(groups, LANES)
    width = halo_send.shape[1]
    piece = shape((8, width))

    packed = call(
        pack_kernel,
        [piece] * 4 + [shape((WORDS * peers, LANES), I32), shape((groups, LANES), I32)],
        [
            pltpu.VMEM((128, WIDE), F32),
            pltpu.VMEM((96, LANES), F32),
            pltpu.VMEM((LANES, LANES), I32),
            pltpu.VMEM((8 * groups, LANES), I32),
        ],
        10**9,
        10**6,
    )(disp, direction, halo_send, masters, send, mortar_count)
    outgoing, words, slots = packed[:4], packed[4], packed[5]

    def exchange(value):
        value = value.reshape(peers, 1, WORDS * LANES)
        value = lax.all_to_all(value, "dom", split_axis=0, concat_axis=0, tiled=True)
        return value.reshape(WORDS * peers, LANES)

    pieces = [shifted(outgoing[o], "dom", moves[o]) for o in range(4)]
    arrived = exchange(words)

    block = 4 * LANES
    steps = pairs // block
    mortar_spec = pl.BlockSpec((QUADS, 36, block), lambda i: (0, 0, i))
    row_spec = pl.BlockSpec((24, block), lambda i: (0, i))
    word_spec = pl.BlockSpec((4 * 4 * WORDS, LANES), lambda i: (i, 0))

    near = call(
        near_kernel,
        shape((24, pairs)),
        [
            pltpu.VMEM((128, WIDE), F32),
            pltpu.VMEM((96, LANES), F32),
            pltpu.VMEM((160, LANES), BF16),
        ],
        10**9,
        6 * 10**6,
        grid=(steps,),
        in_specs=[
            whole(disp.shape),
            whole(direction.shape),
            whole(slaves.shape),
            whole(pair.shape),
            mortar_spec,
            pl.BlockSpec((QUADS, block), lambda i: (0, i)),
        ],
        out_specs=row_spec,
    )(disp, direction, slaves, pair, slave_mortar, gap_offset)

    vmem = pl.BlockSpec(memory_space=pltpu.VMEM)
    element = call(
        element_kernel,
        [shape((128, WIDE))] + [piece] * 4,
        [
            pltpu.VMEM((160, WIDE), F32),
            pltpu.VMEM((WIDE, 32 * elements), BF16),
            pltpu.VMEM((elements // LANES, 256, LANES), F32),
            pltpu.VMEM((elements // LANES, 256, LANES), F32),
            pltpu.VMEM(blocks.shape, BF16),
            pltpu.VMEM((320, WIDE), F32),
            pltpu.SemaphoreType.DMA((4,)),
        ],
        4 * 10**9,
        10**7,
        in_specs=[vmem] * 7 + [pl.BlockSpec(memory_space=pl.ANY)],
    )(disp, direction, *pieces, elem_nodes, blocks)
    own, sums = element[0], element[1:]
    shared = [shifted(sums[o], "dom", -moves[o]) for o in range(4)]

    back, weights = call(
        far_kernel,
        [shape(words.shape, I32), shape((24, pairs))],
        [pltpu.VMEM((32, LANES), I32), pltpu.VMEM((32, LANES), I32)],
        10**9,
        6 * 10**6,
        grid=(steps,),
        in_specs=[word_spec, row_spec, mortar_spec],
        out_specs=[word_spec, row_spec],
    )(arrived, near, master_mortar)
    returned = exchange(back)

    base = call(
        slave_kernel,
        shape((128, WIDE)),
        [pltpu.VMEM((160, LANES), F32), pltpu.VMEM((96, LANES), F32)],
        10**9,
        6 * 10**6,
        grid=(steps,),
        in_specs=[whole((128, WIDE))]
        + [whole((8, width))] * 4
        + [
            whole(halo_send.shape),
            whole(slaves.shape),
            whole(pair.shape),
            mortar_spec,
            row_spec,
        ],
        out_specs=whole((128, WIDE)),
    )(own, *shared, halo_send, slaves, pair, slave_mortar, weights)

    return call(
        last_kernel,
        [shape(load.shape), shape(load.shape)],
        [
            pltpu.VMEM((8 * groups, LANES), I32),
            pltpu.VMEM((160, pairs), BF16),
            pltpu.VMEM((LANES, pairs), BF16),
            pltpu.VMEM((96, LANES), F32),
        ],
        10**9,
        10**6,
    )(returned, slots, masters, base, load)


def solution(mesh):
    return jax.shard_map(
        on_device,
        mesh=mesh,
        in_specs=(
            P(None, "dom"),
            P(None, "dom"),
            P(None, "dom"),
            P(None, None, "dom"),
            P(None, "dom"),
            P("dom", None),
            P("dom", None),
            P("dom", None),
            P("dom", None, None),
            P("dom", None),
            P("dom"),
            P(None, None, "dom"),
            P(None, None, "dom"),
            P(None, "dom"),
        ),
        out_specs=(P(None, "dom"), P(None, "dom")),
        check_vma=False,
    )
```

```python
import jax
import jax.numpy as jnp
from jax import lax
from jax.experimental import pallas as pl
from jax.experimental.pallas import tpu as pltpu
from jax.sharding import PartitionSpec as P

REACH = 2
F32, BF16, I32 = jnp.float32, jnp.bfloat16, jnp.int32
LANES = 128
WIDE = 256
WORDS = 10
QUADS = 9
CHUNKS = 4
UNROLL = 8
FACE = 12
LIMIT = 32767.0
MIB = 1024 * 1024


def offsets():
    return [move for move in range(-REACH, REACH + 1) if move != 0]


def shifted(value, axis, steps):
    count = lax.axis_size(axis)
    pairs = [(source, (source + steps) % count) for source in range(count)]
    return lax.ppermute(value, axis, pairs)


def indicator(row, count):
    number = lax.broadcasted_iota(I32, (count, row.shape[1]), 0)
    return jnp.where(number == row, 1.0, 0.0).astype(BF16)


def cut(value):
    high = value.astype(BF16)
    return high, (value - high.astype(F32)).astype(BF16)


def choose(wide, group, groups):
    total = jnp.where(group == 0, wide[0:8], 0.0)
    for g in range(1, groups):
        total = total + jnp.where(group == g, wide[8 * g : 8 * g + 8], 0.0)
    return total


def gather(parts, row, groups):
    hits = indicator(row & (WIDE - 1), WIDE)
    wide = jnp.dot(parts[0], hits, preferred_element_type=F32)
    for part in parts[1:]:
        wide = wide + jnp.dot(part, hits, preferred_element_type=F32)
    return choose(wide, row >> 8, groups)


def scatter(value, row, groups):
    high = value.astype(BF16).astype(F32)
    low = value - high
    group = row >> 8
    wide = []
    for g in range(groups):
        here = group == g
        wide += [jnp.where(here, high, 0.0), jnp.where(here, low, 0.0)]
    wide = jnp.concatenate(wide, 0).astype(BF16)
    hits = indicator(row & (WIDE - 1), WIDE)
    return across(wide, hits)


def across(left, right):
    return lax.dot_general(left, right, (((1,), (1,)), ((), ())), preferred_element_type=F32)


def fill_table(table, disp, direction):
    table[...] = jnp.zeros(table.shape, F32)
    for g in range(disp.shape[1] // WIDE):
        table[8 * g : 8 * g + 3, :] = disp[:, WIDE * g : WIDE * g + WIDE]
        table[8 * g + 3 : 8 * g + 6, :] = direction[:, WIDE * g : WIDE * g + WIDE]


def turn(v):
    lane = lax.broadcasted_iota(I32, v[0].shape, 1)
    low = lane < 64
    even = (lane & 32) == 0
    a0 = jnp.where(low, v[0], pltpu.roll(v[2], 64, 1))
    a2 = jnp.where(low, pltpu.roll(v[0], 64, 1), v[2])
    a1 = jnp.where(low, v[1], pltpu.roll(v[3], 64, 1))
    a3 = jnp.where(low, pltpu.roll(v[1], 64, 1), v[3])
    return [
        jnp.where(even, a0, pltpu.roll(a1, 32, 1)),
        jnp.where(even, pltpu.roll(a0, 96, 1), a1),
        jnp.where(even, a2, pltpu.roll(a3, 32, 1)),
        jnp.where(even, pltpu.roll(a2, 96, 1), a3),
    ]


def put_words(out, base, tails, words):
    for b, block in enumerate(turn([words[8 * q : 8 * q + 8] for q in range(4)])):
        out[pl.ds(base + WORDS * b, 8), :] = block
    tails[...] = words[32:40]


def put_tails(out, tails, count):
    for h in range(2):
        rows = turn([tails[pl.ds(4 * h + q, count, stride=8), :] for q in range(4)])
        for b in range(4):
            out[pl.ds(WORDS * b + 8 + h, count, stride=4 * WORDS), :] = rows[b]


def get_tails(source, tails, count):
    for h in range(2):
        rows = turn(
            [source[pl.ds(WORDS * b + 8 + h, count, stride=4 * WORDS), :] for b in range(4)]
        )
        for q in range(4):
            tails[pl.ds(4 * h + q, count, stride=8), :] = rows[q]


def get_words(source, base, tail):
    blocks = turn([source[pl.ds(base + WORDS * b, 8), :] for b in range(4)])
    return jnp.concatenate(blocks + [tail], 0)


def step_of(level):
    return jnp.exp(level.astype(F32) * (0.25 * 0.6931471805599453))


def level_of(values):
    top = jnp.max(jnp.abs(values), axis=0, keepdims=True)
    return jnp.ceil(jnp.log(jnp.maximum(top, 1e-30)) * (4.0 / 0.6931471805599453))


def split_words(words):
    second = (words << 16) >> 16
    first = (words - second) >> 16
    return first, second


def decode(words):
    out = []
    row = lax.broadcasted_iota(I32, (8, LANES), 0)
    halves = split_words(words)
    for half in halves:
        scale = step_of(half[36:37]) * (1.0 / LIMIT)
        value = half.astype(F32) * scale
        out.append(jnp.concatenate([value[:32], jnp.where(row < 4, value[32:40], 0.0)], 0))
    return out[0], out[1], halves[0][37:38].astype(F32)


def encode(values):
    level = level_of(values)
    code = jnp.round(values * (LIMIT / step_of(level)))
    row = lax.broadcasted_iota(I32, values.shape, 0)
    return jnp.where(row == 36, level, code)


def fold2(a, b, distance):
    row = lax.broadcasted_iota(I32, a.shape, 0)
    first = (row & distance) == 0
    return jnp.where(first, a, b) + pltpu.roll(jnp.where(first, b, a), 8 - distance, 0)


def fold(v):
    v = [fold2(v[2 * r], v[2 * r + 1], 1) for r in range(4)]
    v = [fold2(v[2 * r], v[2 * r + 1], 2) for r in range(2)]
    return fold2(v[0], v[1], 4)


def tail_rows(block):
    return jnp.concatenate([block, jnp.zeros((4, LANES), F32)], 0)


def contract(mortar, lane, first, second):
    sums = ([], [])
    for q in range(QUADS):
        pieces = [mortar[q, 8 * t : 8 * t + 8, pl.ds(lane, LANES)] for t in range(4)]
        pieces.append(tail_rows(mortar[q, 32:36, pl.ds(lane, LANES)]))
        for field, out in zip((first, second), sums):
            total = pieces[0] * field[0:8]
            for t in range(1, 5):
                total = total + pieces[t] * field[8 * t : 8 * t + 8]
            out.append(total)
    last = fold2(sums[0][8], sums[1][8], 1)
    last = last + pltpu.roll(last, 6, 0)
    last = last + pltpu.roll(last, 4, 0)
    return fold(sums[0][:8]), fold(sums[1][:8]), last


def adjoint(mortar, lane, weights):
    rows = [(weights[q : q + 1], weights[8 + q : 9 + q]) for q in range(8)]
    rows.append((weights[16:17], weights[17:18]))
    sums = []
    for t in range(5):
        pair = [None, None]
        for q in range(QUADS):
            if t < 4:
                piece = mortar[q, 8 * t : 8 * t + 8, pl.ds(lane, LANES)]
            else:
                piece = tail_rows(mortar[q, 32:36, pl.ds(lane, LANES)])
            for w in range(2):
                term = piece * rows[q][w]
                pair[w] = term if q == 0 else pair[w] + term
        sums.append(pair)
    return [jnp.concatenate([pair[w] for pair in sums], 0) for w in range(2)]


def fill_faces(faces, parts, nodes):
    for a in range(FACE):
        faces[pl.ds(a, 8, stride=FACE), :] = gather(parts, nodes[a : a + 1, :], 16)


def padded_fields(faces):
    pad = jnp.zeros((4, LANES), F32)
    return jnp.concatenate([faces[0:36], pad], 0), jnp.concatenate([faces[36:72], pad], 0)


def pack_kernel(disp, direction, halo, nodes, send, count, s0, s1, s2, s3, out, slots, table, faces, square, tails):
    fill_table(table, disp, direction)
    parts = cut(table[...])
    for o, piece in enumerate((s0, s1, s2, s3)):
        piece[...] = gather(parts[:1], halo[o : o + 1, :], 16)
    fill_faces(faces, parts, nodes)
    first, second = padded_fields(faces)
    row = lax.broadcasted_iota(I32, first.shape, 0)
    codes = [encode(first), encode(second)]
    codes[0] = jnp.where(row == 37, 1.0, codes[0])
    left = []
    for code in codes:
        high = jnp.floor(code * (1.0 / 256.0))
        left += [high, code - 256.0 * high]
    left = jnp.concatenate(left, 0).astype(BF16)
    square[...] = jnp.zeros(square.shape, I32)
    square[0:32, :] = send[...]
    square[32:33, :] = count[...]
    turned = square[...].T
    lane = lax.broadcasted_iota(I32, turned.shape, 1)
    square[...] = jnp.where(lane < turned[:, 32:33], turned, -1)
    lane = lax.broadcasted_iota(I32, (32, LANES), 1)
    rows = square[pl.ds(0, 32, stride=4), :]
    for b in range(1, 4):
        moved = pltpu.roll(square[pl.ds(b, 32, stride=4), :], 32 * b, 1)
        rows = jnp.where((lane >> 5) == b, moved, rows)
    slots[...] = rows

    def group_pair(i, carry):
        hits = [indicator(slots[pl.ds(2 * i + t, 1), :], LANES) for t in range(2)]
        wide = jnp.dot(left, jnp.concatenate(hits, 1), preferred_element_type=F32)
        for t in range(2):
            here = wide[:, LANES * t : LANES * t + LANES]
            first = (here[0:40] * 256.0 + here[40:80]).astype(I32)
            second = (here[80:120] * 256.0 + here[120:160]).astype(I32)
            base = pl.multiple_of(80 * i, 8) + 40 * t
            at = pl.multiple_of(16 * i, 8) + 8 * t
            put_words(out, base, tails.at[pl.ds(at, 8), :], (first << 16) + second)
        return carry

    lax.fori_loop(0, 16, group_pair, 0, unroll=True)
    put_tails(out, tails, 32)


def element_kernel(disp, direction, p0, p1, p2, p3, nodes, blocks, own, s0, s1, s2, s3, table, hits, x, y, held, sums, sems):
    chunk = blocks.shape[0] // sems.shape[0]
    copies = [
        pltpu.make_async_copy(
            blocks.at[pl.ds(chunk * n, chunk)], held.at[pl.ds(chunk * n, chunk)], sems.at[n]
        )
        for n in range(sems.shape[0])
    ]
    for copy in copies:
        copy.start()
    fill_table(table, disp, direction)
    for o, piece in enumerate((p0, p1, p2, p3)):
        table[8 * (16 + o) : 8 * (17 + o), :] = piece[...]
    coarse = table[...].astype(BF16)
    elements = nodes.shape[1]

    def gather_node(a, carry):
        for h in range(elements // WIDE):
            row = nodes[pl.ds(a, 1), WIDE * h : WIDE * h + WIDE]
            hit = indicator(row & (WIDE - 1), WIDE)
            at = pl.multiple_of(a * elements, WIDE) + WIDE * h
            hits[:, pl.ds(at, WIDE)] = hit
            wide = jnp.dot(coarse, hit, preferred_element_type=F32)
            picked = choose(wide, row >> 8, 20)
            for part in range(WIDE // LANES):
                x[2 * h + part, pl.ds(a, 8, stride=32), :] = picked[
                    :, LANES * part : LANES * part + LANES
                ]
        return carry

    lax.fori_loop(0, 32, gather_node, 0, unroll=8)
    y[...] = jnp.zeros(y.shape, F32)
    for n, copy in enumerate(copies):
        copy.wait()
        for part in range(elements // LANES):

            def eight_rows(i, carry, part=part, n=n):
                u, v = [], []
                for r in range(8):
                    block = held[
                        chunk * n + 8 * i + r, :, LANES * part : LANES * part + LANES
                    ].astype(F32)
                    for w, out in enumerate((u, v)):
                        total = block[0:8] * x[part, 96 * w : 96 * w + 8, :]
                        for t in range(1, 12):
                            total = total + block[8 * t : 8 * t + 8] * x[
                                part, 96 * w + 8 * t : 96 * w + 8 * t + 8, :
                            ]
                        out.append(total)
                at = pl.multiple_of(chunk * n + 8 * i, 8)
                y[part, pl.ds(at, 8), :] = fold(u)
                y[part, pl.ds(96 + at, 8), :] = fold(v)
                return carry

            lax.fori_loop(0, chunk // 8, eight_rows, 0)
    sums[...] = jnp.zeros(sums.shape, F32)

    def scatter_node(a, carry):
        for h in range(elements // WIDE):
            row = nodes[pl.ds(a, 1), WIDE * h : WIDE * h + WIDE] >> 8
            value = jnp.concatenate(
                [y[2 * h + part, pl.ds(a, 8, stride=32), :] for part in range(2)], 1
            )
            high = value.astype(BF16).astype(F32)
            low = value - high
            wide = []
            for g in range(20):
                here = row == g
                wide += [jnp.where(here, high, 0.0), jnp.where(here, low, 0.0)]
            wide = jnp.concatenate(wide, 0).astype(BF16)
            at = pl.multiple_of(a * elements, WIDE) + WIDE * h
            sums[...] += across(wide, hits[:, pl.ds(at, WIDE)])
        return carry

    lax.fori_loop(0, 32, scatter_node, 0, unroll=8)
    for g in range(16):
        own[8 * g : 8 * g + 8, :] = sums[16 * g : 16 * g + 8, :] + sums[16 * g + 8 : 16 * g + 16, :]
    for o, piece in enumerate((s0, s1, s2, s3)):
        g = 16 + o
        piece[...] = sums[16 * g : 16 * g + 8, :] + sums[16 * g + 8 : 16 * g + 16, :]


def fetch(source, held, sems):
    count = sems.shape[0]
    part = source.shape[2] // count
    copies = []
    for n in range(count):
        at = pl.ds(part * n, part)
        copies.append(pltpu.make_async_copy(source.at[:, :, at], held.at[:, :, at], sems.at[n]))
        copies[-1].start()
    return copies


def over_groups(copies, groups, body):
    part = groups // len(copies)
    for n, copy in enumerate(copies):
        copy.wait()

        def step(i, carry, n=n):
            body(part * n + i, pl.multiple_of(LANES * (part * n + i), LANES))
            return carry

        lax.fori_loop(0, part, step, 0, unroll=UNROLL)


def near_kernel(disp, direction, nodes, pair, gap, source, out, table, faces, fields, mortar, sems):
    copies = fetch(source, mortar, sems)
    fill_table(table, disp, direction)
    fill_faces(faces, cut(table[...]), nodes)
    left = jnp.concatenate(cut(jnp.concatenate(padded_fields(faces), 0)), 0)
    groups = out.shape[1] // LANES
    for i in range(groups // 2):
        hits = [indicator(pair[2 * i + t : 2 * i + t + 1, :], LANES) for t in range(2)]
        wide = jnp.dot(left, jnp.concatenate(hits, 1), preferred_element_type=F32)
        fields[:, 2 * LANES * i : 2 * LANES * (i + 1)] = wide[:80] + wide[80:]
    number = lax.broadcasted_iota(I32, (8, LANES), 0)

    def group(g, lane):
        at = pl.ds(lane, LANES)
        opening, tangent, last = contract(mortar, lane, fields.at[0:40, at], fields.at[40:80, at])
        out[0:8, at] = opening + gap[0:8, at]
        out[8:16, at] = tangent
        out[16:24, at] = last + jnp.where((number & 1) == 0, gap[8:9, at], 0.0)

    over_groups(copies, groups, group)

def react(opening, tangent, live):
    fade = jnp.exp(-jnp.abs(opening))
    pressure = jnp.maximum(opening, 0.0) + jnp.log1p(fade)
    share = jnp.where(opening >= 0.0, 1.0, fade) / (1.0 + fade)
    return pressure * live, share * tangent * live


def far_kernel(arrived, near, p0, p1, p2, p3, source, out, weights, tails, back, mortar, sems):
    copies = fetch(source, mortar, sems)
    groups = near.shape[1] // LANES
    get_tails(arrived, tails, groups)
    number = lax.broadcasted_iota(I32, (8, LANES), 0)

    def group(g, lane):
        at = pl.ds(lane, LANES)
        base = pl.multiple_of(40 * g, 8)
        eight = pl.ds(pl.multiple_of(8 * g, 8), 8)
        first, second, live = decode(get_words(arrived, base, tails[eight, :]))
        opening, tangent, last = contract(mortar, lane, first, second)
        opening = opening + near[0:8, at]
        tangent = tangent + near[8:16, at]
        last = last + near[16:24, at]
        pressure, increment = react(opening, tangent, live)
        ninth = react(last[0:1], last[1:2], live)
        ninth = jnp.where((number & 1) == 0, ninth[0], ninth[1])
        here = jnp.concatenate([pressure, increment, ninth], 0)
        weights[:, at] = here
        first, second = (encode(force).astype(I32) for force in adjoint(mortar, lane, here))
        put_words(out, base, back.at[eight, :], (first << 16) + second)

    over_groups(copies, groups, group)
    put_tails(out, back, groups)

def add_faces(faces, nodes):
    total = None
    for a in range(FACE):
        term = scatter(faces[pl.ds(a, 8, stride=FACE), :], nodes[a : a + 1, :], 16)
        total = term if a == 0 else total + term
    return total


def merge(total, groups):
    return [total[16 * g : 16 * g + 8] + total[16 * g + 8 : 16 * g + 16] for g in range(groups)]


def slave_kernel(own, nodes, pair, weights, source, out, forces, hits, faces, mortar, sems):
    copies = fetch(source, mortar, sems)
    groups = weights.shape[1] // LANES

    def group(g, lane):
        at = pl.ds(lane, LANES)
        force = jnp.concatenate(adjoint(mortar, lane, weights[:, at]), 0)
        forces[:, at] = jnp.concatenate(cut(force), 0)
        hits[:, at] = indicator(pair[pl.ds(g, 1), :], LANES)

    over_groups(copies, groups, group)
    sums = across(forces[...], hits[...])
    for g, rows in enumerate(merge(face_sums(sums, faces, nodes), 16)):
        out[8 * g : 8 * g + 8, :] = own[8 * g : 8 * g + 8, :] + rows


def face_sums(sums, faces, nodes):
    faces[...] = jnp.zeros(faces.shape, F32)
    faces[0:36, :] = sums[0:36] + sums[80:116]
    faces[36:72, :] = sums[40:76] + sums[120:156]
    return add_faces(faces, nodes)

def last_kernel(arrived, slots, nodes, base, p0, p1, p2, p3, halo, load, residual, applied, tails, forces, hits, faces):
    get_tails(arrived, tails, 32)

    def group(i, carry):
        at = pl.multiple_of(8 * i, 8)
        words = get_words(arrived, pl.multiple_of(40 * i, 8), tails[pl.ds(at, 8), :])
        first, second, _ = decode(words)
        force = jnp.concatenate([first, second], 0)
        lane = pl.multiple_of(LANES * i, LANES)
        forces[:, pl.ds(lane, LANES)] = jnp.concatenate(cut(force), 0)
        hits[:, pl.ds(lane, LANES)] = indicator(slots[pl.ds(i, 1), :], LANES)
        return carry

    lax.fori_loop(0, 32, group, 0, unroll=16)
    total = face_sums(across(forces[...], hits[...]), faces, nodes)
    for o, piece in enumerate((p0, p1, p2, p3)):
        total = total + scatter(piece[...], halo[o : o + 1, :], 16)
    for g, rows in enumerate(merge(total, 16)):
        rows = rows + base[8 * g : 8 * g + 8, :]
        at = WIDE * g
        residual[:, at : at + WIDE] = load[:, at : at + WIDE] - rows[0:3]
        applied[:, at : at + WIDE] = rows[3:6]


def shape(dims, kind=F32):
    return jax.ShapeDtypeStruct(dims, kind)


def settled(*arrays):
    return [pltpu.with_memory_space_constraint(array, pltpu.HBM) for array in arrays]


def call(kernel, results, scratch, flops, size, room, **extra):
    return pl.pallas_call(
        kernel,
        out_shape=results,
        scratch_shapes=scratch,
        compiler_params=pltpu.CompilerParams(vmem_limit_bytes=room * MIB),
        cost_estimate=pl.CostEstimate(flops=flops, bytes_accessed=size, transcendentals=0),
        **extra,
    )


def pack(disp, direction, halo_send, masters, send, count):
    groups = send.shape[1] // 4
    piece = shape((8, halo_send.shape[1]))
    return call(
        pack_kernel,
        [piece] * 4 + [shape((WORDS * send.shape[1], LANES), I32), shape((groups, LANES), I32)],
        [
            pltpu.VMEM((128, WIDE), F32),
            pltpu.VMEM((96, LANES), F32),
            pltpu.VMEM((LANES, LANES), I32),
            pltpu.VMEM((8 * groups, LANES), I32),
        ],
        10**9,
        10**6,
        8,
    )(*settled(disp, direction, halo_send, masters, send, count))


def inputs(count):
    vmem = pl.BlockSpec(memory_space=pltpu.VMEM)
    return [vmem] * count + [pl.BlockSpec(memory_space=pl.ANY)]


def mortar_scratch(mortar):
    return [pltpu.VMEM(mortar.shape, F32), pltpu.SemaphoreType.DMA((CHUNKS,))]


def near_part(disp, direction, slaves, pair, mortar, gap):
    pairs = mortar.shape[2]
    return call(
        near_kernel,
        shape((24, pairs)),
        [
            pltpu.VMEM((128, WIDE), F32),
            pltpu.VMEM((96, LANES), F32),
            pltpu.VMEM((80, pairs), F32),
        ]
        + mortar_scratch(mortar),
        10**9,
        6 * 10**6,
        14,
        in_specs=inputs(5),
    )(*settled(disp, direction, slaves, pair, gap, mortar))


def elements_part(disp, direction, pieces, nodes, blocks):
    elements = nodes.shape[1]
    return call(
        element_kernel,
        [shape((128, WIDE))] + [shape((8, WIDE))] * 4,
        [
            pltpu.VMEM((160, WIDE), F32),
            pltpu.VMEM((WIDE, 32 * elements), BF16),
            pltpu.VMEM((elements // LANES, 256, LANES), F32),
            pltpu.VMEM((elements // LANES, 256, LANES), F32),
            pltpu.VMEM(blocks.shape, BF16),
            pltpu.VMEM((320, WIDE), F32),
            pltpu.SemaphoreType.DMA((4,)),
        ],
        4 * 10**9,
        10**7,
        32,
        in_specs=inputs(7),
    )(*settled(disp, direction), *pieces, *settled(nodes, blocks))


def far_part(arrived, near, mortar, pieces):
    pairs = mortar.shape[2]
    tails = pltpu.VMEM((8 * (pairs // LANES), LANES), I32)
    return call(
        far_kernel,
        [shape(arrived.shape, I32), shape((24, pairs))],
        [tails, tails] + mortar_scratch(mortar),
        10**9,
        6 * 10**6,
        14,
        in_specs=inputs(6),
    )(arrived, near, *pieces, *settled(mortar))


def sum_scratch(pairs):
    return [
        pltpu.VMEM((160, pairs), BF16),
        pltpu.VMEM((LANES, pairs), BF16),
        pltpu.VMEM((96, LANES), F32),
    ]


def slave_part(own, slaves, pair, mortar, weights):
    pairs = mortar.shape[2]
    return call(
        slave_kernel,
        shape((128, WIDE)),
        sum_scratch(pairs) + mortar_scratch(mortar),
        10**9,
        6 * 10**6,
        14,
        in_specs=inputs(4),
    )(own, *settled(slaves, pair), weights, *settled(mortar))


def last_part(returned, slots, masters, base, shared, halo_send, load):
    groups = slots.shape[0]
    return call(
        last_kernel,
        [shape(load.shape), shape(load.shape)],
        [pltpu.VMEM((8 * groups, LANES), I32)] + sum_scratch(groups * LANES),
        10**9,
        10**6,
        10,
    )(returned, slots, *settled(masters), base, *shared, *settled(halo_send, load))


def on_device(
    disp,
    direction,
    load,
    blocks,
    elem_nodes,
    halo_send,
    master_nodes,
    slave_nodes,
    mortar_send,
    mortar_count,
    pair_slave,
    slave_mortar,
    master_mortar,
    gap_offset,
):
    peers = lax.axis_size("dom")
    moves = offsets()
    masters, slaves = master_nodes.T, slave_nodes.T
    send = mortar_send[0].T
    pair = pair_slave.reshape(-1, LANES)

    def exchange(value):
        value = value.reshape(peers, 1, WORDS * LANES)
        value = lax.all_to_all(value, "dom", split_axis=0, concat_axis=0, tiled=True)
        return value.reshape(WORDS * peers, LANES)

    packed = pack(disp, direction, halo_send, masters, send, mortar_count)
    outgoing, words, slots = packed[:4], packed[4], packed[5]
    arrived = exchange(words)
    pieces = [shifted(outgoing[o], "dom", moves[o]) for o in range(4)]
    near = near_part(disp, direction, slaves, pair, slave_mortar, gap_offset)
    element = elements_part(disp, direction, pieces, elem_nodes, blocks)
    own, sums = element[0], element[1:]
    shared = [shifted(sums[o], "dom", -moves[o]) for o in range(4)]
    back, weights = far_part(arrived, near, master_mortar, pieces)
    returned = exchange(back)
    base = slave_part(own, slaves, pair, slave_mortar, weights)
    return last_part(returned, slots, masters, base, shared, halo_send, load)


def solution(mesh):
    return jax.shard_map(
        on_device,
        mesh=mesh,
        in_specs=(
            P(None, "dom"),
            P(None, "dom"),
            P(None, "dom"),
            P(None, None, "dom"),
            P(None, "dom"),
            P("dom", None),
            P("dom", None),
            P("dom", None),
            P("dom", None, None),
            P("dom", None),
            P("dom"),
            P(None, None, "dom"),
            P(None, None, "dom"),
            P(None, "dom"),
        ),
        out_specs=(P(None, "dom"), P(None, "dom")),
        check_vma=False,
    )
```

```python
import jax
import jax.numpy as jnp
from jax import lax
from jax.experimental import pallas as pl
from jax.experimental.pallas import tpu as pltpu
from jax.sharding import PartitionSpec as P

REACH = 2
F32, BF16, I32 = jnp.float32, jnp.bfloat16, jnp.int32
LANES = 128
WIDE = 256
WORDS = 10
QUADS = 9
FACE = 12
LIMIT = 32767.0
MIB = 1024 * 1024


def offsets():
    return [move for move in range(-REACH, REACH + 1) if move != 0]


def shifted(value, axis, steps):
    count = lax.axis_size(axis)
    pairs = [(source, (source + steps) % count) for source in range(count)]
    return lax.ppermute(value, axis, pairs)


def indicator(row, count):
    number = lax.broadcasted_iota(jnp.int16, (count, row.shape[1]), 0)
    return jnp.where(number == row.astype(jnp.int16), jnp.ones((), BF16), jnp.zeros((), BF16))


def cut(value):
    high = value.astype(BF16)
    return high, (value - high.astype(F32)).astype(BF16)


def choose(wide, group, groups):
    total = jnp.where(group == 0, wide[0:8], 0.0)
    for g in range(1, groups):
        total = total + jnp.where(group == g, wide[8 * g : 8 * g + 8], 0.0)
    return total


def gather(parts, row, groups):
    hits = indicator(row & (WIDE - 1), WIDE)
    wide = jnp.dot(parts[0], hits, preferred_element_type=F32)
    for part in parts[1:]:
        wide = wide + jnp.dot(part, hits, preferred_element_type=F32)
    return choose(wide, row >> 8, groups)


def place(value, group, groups):
    both = jnp.concatenate(cut(value), 0)
    group = jnp.broadcast_to(group, both.shape).astype(jnp.int16)
    zero = jnp.zeros(both.shape, BF16)
    return jnp.concatenate([jnp.where(group == g, both, zero) for g in range(groups)], 0)


def scatter(value, row, groups):
    wide = place(value, row >> 8, groups)
    hits = indicator(row & (WIDE - 1), WIDE)
    return across(wide, hits)


def across(left, right):
    return lax.dot_general(left, right, (((1,), (1,)), ((), ())), preferred_element_type=F32)


def fill_table(table, disp, direction):
    table[...] = jnp.zeros(table.shape, F32)
    for g in range(disp.shape[1] // WIDE):
        table[8 * g : 8 * g + 3, :] = disp[:, WIDE * g : WIDE * g + WIDE]
        table[8 * g + 3 : 8 * g + 6, :] = direction[:, WIDE * g : WIDE * g + WIDE]


def turn(v):
    lane = lax.broadcasted_iota(I32, v[0].shape, 1)
    low = lane < 64
    even = (lane & 32) == 0
    a0 = jnp.where(low, v[0], pltpu.roll(v[2], 64, 1))
    a2 = jnp.where(low, pltpu.roll(v[0], 64, 1), v[2])
    a1 = jnp.where(low, v[1], pltpu.roll(v[3], 64, 1))
    a3 = jnp.where(low, pltpu.roll(v[1], 64, 1), v[3])
    return [
        jnp.where(even, a0, pltpu.roll(a1, 32, 1)),
        jnp.where(even, pltpu.roll(a0, 96, 1), a1),
        jnp.where(even, a2, pltpu.roll(a3, 32, 1)),
        jnp.where(even, pltpu.roll(a2, 96, 1), a3),
    ]


def put_words(out, base, tails, words):
    for b, block in enumerate(turn([words[8 * q : 8 * q + 8] for q in range(4)])):
        out[pl.ds(base + WORDS * b, 8), :] = block
    tails[...] = words[32:40]


def put_tails(out, tails, count):
    for h in range(2):
        rows = turn([tails[pl.ds(4 * h + q, count, stride=8), :] for q in range(4)])
        for b in range(4):
            out[pl.ds(WORDS * b + 8 + h, count, stride=4 * WORDS), :] = rows[b]


def get_tails(source, tails, count):
    for h in range(2):
        rows = turn(
            [source[pl.ds(WORDS * b + 8 + h, count, stride=4 * WORDS), :] for b in range(4)]
        )
        for q in range(4):
            tails[pl.ds(4 * h + q, count, stride=8), :] = rows[q]


def get_words(source, base, tail):
    blocks = turn([source[pl.ds(base + WORDS * b, 8), :] for b in range(4)])
    return jnp.concatenate(blocks + [tail], 0)


def step_of(level):
    return jnp.exp(level.astype(F32) * (0.25 * 0.6931471805599453))


def level_of(values):
    top = jnp.max(jnp.abs(values), axis=0, keepdims=True)
    return jnp.ceil(jnp.log(jnp.maximum(top, 1e-30)) * (4.0 / 0.6931471805599453))


def split_words(words):
    second = (words << 16) >> 16
    first = (words - second) >> 16
    return first, second


def decode(words):
    out = []
    row = lax.broadcasted_iota(I32, (8, LANES), 0)
    halves = split_words(words)
    for half in halves:
        scale = step_of(half[36:37]) * (1.0 / LIMIT)
        value = half.astype(F32) * scale
        out.append(jnp.concatenate([value[:32], jnp.where(row < 4, value[32:40], 0.0)], 0))
    return out[0], out[1], halves[0][37:38].astype(F32)


def encode(values):
    level = level_of(values)
    code = jnp.round(values * (LIMIT / step_of(level)))
    row = lax.broadcasted_iota(I32, values.shape, 0)
    return jnp.where(row == 36, level, code)


def fold2(a, b, distance):
    row = lax.broadcasted_iota(I32, a.shape, 0)
    first = (row & distance) == 0
    return jnp.where(first, a, b) + pltpu.roll(jnp.where(first, b, a), 8 - distance, 0)


def fold(v):
    v = [fold2(v[2 * r], v[2 * r + 1], 1) for r in range(4)]
    v = [fold2(v[2 * r], v[2 * r + 1], 2) for r in range(2)]
    return fold2(v[0], v[1], 4)


def tail_rows(block):
    return jnp.concatenate([block, jnp.zeros((4, LANES), F32)], 0)


def contract(mortar, lane, first, second):
    sums = ([], [])
    for q in range(QUADS):
        pieces = [mortar[q, 8 * t : 8 * t + 8, pl.ds(lane, LANES)] for t in range(4)]
        pieces.append(tail_rows(mortar[q, 32:36, pl.ds(lane, LANES)]))
        for field, out in zip((first, second), sums):
            total = pieces[0] * field[0:8]
            for t in range(1, 5):
                total = total + pieces[t] * field[8 * t : 8 * t + 8]
            out.append(total)
    last = fold2(sums[0][8], sums[1][8], 1)
    last = last + pltpu.roll(last, 6, 0)
    last = last + pltpu.roll(last, 4, 0)
    return fold(sums[0][:8]), fold(sums[1][:8]), last


def adjoint(mortar, lane, weights):
    rows = [(weights[q : q + 1], weights[8 + q : 9 + q]) for q in range(8)]
    rows.append((weights[16:17], weights[17:18]))
    sums = []
    for t in range(5):
        pair = [None, None]
        for q in range(QUADS):
            if t < 4:
                piece = mortar[q, 8 * t : 8 * t + 8, pl.ds(lane, LANES)]
            else:
                piece = tail_rows(mortar[q, 32:36, pl.ds(lane, LANES)])
            for w in range(2):
                term = piece * rows[q][w]
                pair[w] = term if q == 0 else pair[w] + term
        sums.append(pair)
    return [jnp.concatenate([pair[w] for pair in sums], 0) for w in range(2)]


def fill_faces(faces, parts, nodes):
    for a in range(FACE):
        faces[pl.ds(a, 8, stride=FACE), :] = gather(parts, nodes[a : a + 1, :], 16)


def padded_fields(faces):
    pad = jnp.zeros((4, LANES), F32)
    return jnp.concatenate([faces[0:36], pad], 0), jnp.concatenate([faces[36:72], pad], 0)


def pack_kernel(disp, direction, halo, nodes, send, count, s0, s1, s2, s3, out, slots, table, faces, square, tails):
    fill_table(table, disp, direction)
    parts = cut(table[...])
    for o, piece in enumerate((s0, s1, s2, s3)):
        piece[...] = gather(parts[:1], halo[o : o + 1, :], 16)
    fill_faces(faces, parts, nodes)
    first, second = padded_fields(faces)
    row = lax.broadcasted_iota(I32, first.shape, 0)
    codes = [encode(first), encode(second)]
    codes[0] = jnp.where(row == 37, 1.0, codes[0])
    left = []
    for code in codes:
        high = jnp.floor(code * (1.0 / 256.0))
        left += [high, code - 256.0 * high]
    left = jnp.concatenate(left, 0).astype(BF16)
    square[...] = jnp.zeros(square.shape, I32)
    square[0:32, :] = send[...]
    square[32:33, :] = count[...]
    turned = square[...].T
    lane = lax.broadcasted_iota(I32, turned.shape, 1)
    square[...] = jnp.where(lane < turned[:, 32:33], turned, -1)
    lane = lax.broadcasted_iota(I32, (32, LANES), 1)
    rows = square[pl.ds(0, 32, stride=4), :]
    for b in range(1, 4):
        moved = pltpu.roll(square[pl.ds(b, 32, stride=4), :], 32 * b, 1)
        rows = jnp.where((lane >> 5) == b, moved, rows)
    slots[...] = rows

    def group_pair(i, carry):
        hits = [indicator(slots[pl.ds(2 * i + t, 1), :], LANES) for t in range(2)]
        wide = jnp.dot(left, jnp.concatenate(hits, 1), preferred_element_type=F32)
        for t in range(2):
            here = wide[:, LANES * t : LANES * t + LANES]
            first = (here[0:40] * 256.0 + here[40:80]).astype(I32)
            second = (here[80:120] * 256.0 + here[120:160]).astype(I32)
            base = pl.multiple_of(80 * i, 8) + 40 * t
            at = pl.multiple_of(16 * i, 8) + 8 * t
            put_words(out, base, tails.at[pl.ds(at, 8), :], (first << 16) + second)
        return carry

    lax.fori_loop(0, 16, group_pair, 0, unroll=True)
    put_tails(out, tails, 32)


def element_kernel(disp, direction, p0, p1, p2, p3, nodes, blocks, own, s0, s1, s2, s3, table, hits, x, y, held, sums, sems):
    chunk = blocks.shape[0] // sems.shape[0]
    copies = [
        pltpu.make_async_copy(
            blocks.at[pl.ds(chunk * n, chunk)], held.at[pl.ds(chunk * n, chunk)], sems.at[n]
        )
        for n in range(sems.shape[0])
    ]
    for copy in copies:
        copy.start()
    fill_table(table, disp, direction)
    for o, piece in enumerate((p0, p1, p2, p3)):
        table[8 * (16 + o) : 8 * (17 + o), :] = piece[...]
    coarse = table[...].astype(BF16)
    elements = nodes.shape[1]

    def gather_node(a, carry):
        for h in range(elements // WIDE):
            row = nodes[pl.ds(a, 1), WIDE * h : WIDE * h + WIDE]
            hit = indicator(row & (WIDE - 1), WIDE)
            at = pl.multiple_of(a * elements, WIDE) + WIDE * h
            hits[:, pl.ds(at, WIDE)] = hit
            wide = jnp.dot(coarse, hit, preferred_element_type=F32)
            picked = choose(wide, row >> 8, 20)
            for part in range(WIDE // LANES):
                x[2 * h + part, pl.ds(a, 8, stride=32), :] = picked[
                    :, LANES * part : LANES * part + LANES
                ]
        return carry

    lax.fori_loop(0, 32, gather_node, 0, unroll=8)
    y[:, 192:256, :] = jnp.zeros((y.shape[0], 64, LANES), F32)
    for n, copy in enumerate(copies):
        copy.wait()
        for part in range(elements // LANES):

            def eight_rows(i, carry, part=part, n=n):
                u, v = [], []
                for r in range(8):
                    block = held[
                        chunk * n + 8 * i + r, :, LANES * part : LANES * part + LANES
                    ].astype(F32)
                    for w, out in enumerate((u, v)):
                        total = block[0:8] * x[part, 96 * w : 96 * w + 8, :]
                        for t in range(1, 12):
                            total = total + block[8 * t : 8 * t + 8] * x[
                                part, 96 * w + 8 * t : 96 * w + 8 * t + 8, :
                            ]
                        out.append(total)
                at = pl.multiple_of(chunk * n + 8 * i, 8)
                y[part, pl.ds(at, 8), :] = fold(u)
                y[part, pl.ds(96 + at, 8), :] = fold(v)
                return carry

            lax.fori_loop(0, chunk // 8, eight_rows, 0, unroll=3)
    sums[...] = jnp.zeros(sums.shape, F32)

    def scatter_node(a, carry):
        for h in range(elements // WIDE):
            row = nodes[pl.ds(a, 1), WIDE * h : WIDE * h + WIDE] >> 8
            value = jnp.concatenate(
                [y[2 * h + part, pl.ds(a, 8, stride=32), :] for part in range(2)], 1
            )
            wide = place(value, row, 20)
            at = pl.multiple_of(a * elements, WIDE) + WIDE * h
            sums[...] += across(wide, hits[:, pl.ds(at, WIDE)])
        return carry

    lax.fori_loop(0, 32, scatter_node, 0, unroll=8)
    for g in range(16):
        own[8 * g : 8 * g + 8, :] = sums[16 * g : 16 * g + 8, :] + sums[16 * g + 8 : 16 * g + 16, :]
    for o, piece in enumerate((s0, s1, s2, s3)):
        g = 16 + o
        piece[...] = sums[16 * g : 16 * g + 8, :] + sums[16 * g + 8 : 16 * g + 16, :]


def fetch(source, held, sems):
    count = sems.shape[0]
    part = source.shape[2] // count
    copies = []
    for n in range(count):
        at = pl.ds(part * n, part)
        copies.append(pltpu.make_async_copy(source.at[:, :, at], held.at[:, :, at], sems.at[n]))
        copies[-1].start()
    return copies


def over_groups(copies, groups, body):
    part = groups // len(copies)
    for n, copy in enumerate(copies):
        copy.wait()

        def step(i, carry, n=n):
            body(part * n + i, pl.multiple_of(LANES * (part * n + i), LANES))
            return carry

        lax.fori_loop(0, part, step, 0, unroll=True)


def near_kernel(disp, direction, nodes, pair, gap, source, out, table, faces, fields, mortar, sems):
    copies = fetch(source, mortar, sems)
    fill_table(table, disp, direction)
    fill_faces(faces, cut(table[...]), nodes)
    left = jnp.concatenate(cut(jnp.concatenate(padded_fields(faces), 0)), 0)
    groups = out.shape[1] // LANES
    for i in range(groups // 2):
        hits = [indicator(pair[2 * i + t : 2 * i + t + 1, :], LANES) for t in range(2)]
        wide = jnp.dot(left, jnp.concatenate(hits, 1), preferred_element_type=F32)
        fields[:, 2 * LANES * i : 2 * LANES * (i + 1)] = wide[:80] + wide[80:]
    number = lax.broadcasted_iota(I32, (8, LANES), 0)

    def group(g, lane):
        at = pl.ds(lane, LANES)
        opening, tangent, last = contract(mortar, lane, fields.at[0:40, at], fields.at[40:80, at])
        out[0:8, at] = opening + gap[0:8, at]
        out[8:16, at] = tangent
        out[16:24, at] = last + jnp.where((number & 1) == 0, gap[8:9, at], 0.0)

    over_groups(copies, groups, group)

def react(opening, tangent, live):
    fade = jnp.exp(-jnp.abs(opening))
    pressure = jnp.maximum(opening, 0.0) + jnp.log1p(fade)
    share = jnp.where(opening >= 0.0, 1.0, fade) / (1.0 + fade)
    return pressure * live, share * tangent * live


def far_kernel(arrived, near, p0, p1, p2, p3, source, out, weights, tails, back, mortar, sems):
    copies = fetch(source, mortar, sems)
    groups = near.shape[1] // LANES
    get_tails(arrived, tails, groups)
    number = lax.broadcasted_iota(I32, (8, LANES), 0)

    def group(g, lane):
        at = pl.ds(lane, LANES)
        base = pl.multiple_of(40 * g, 8)
        eight = pl.ds(pl.multiple_of(8 * g, 8), 8)
        first, second, live = decode(get_words(arrived, base, tails[eight, :]))
        opening, tangent, last = contract(mortar, lane, first, second)
        opening = opening + near[0:8, at]
        tangent = tangent + near[8:16, at]
        last = last + near[16:24, at]
        pressure, increment = react(opening, tangent, live)
        ninth = react(last[0:1], last[1:2], live)
        ninth = jnp.where((number & 1) == 0, ninth[0], ninth[1])
        here = jnp.concatenate([pressure, increment, ninth], 0)
        weights[:, at] = here
        first, second = (encode(force).astype(I32) for force in adjoint(mortar, lane, here))
        put_words(out, base, back.at[eight, :], (first << 16) + second)

    over_groups(copies, groups, group)
    put_tails(out, back, groups)

def add_faces(faces, nodes):
    total = None
    for a in range(FACE):
        term = scatter(faces[pl.ds(a, 8, stride=FACE), :], nodes[a : a + 1, :], 16)
        total = term if a == 0 else total + term
    return total


def merge(total, groups):
    return [total[16 * g : 16 * g + 8] + total[16 * g + 8 : 16 * g + 16] for g in range(groups)]


def slave_kernel(own, nodes, pair, weights, source, out, forces, hits, faces, mortar, sems):
    copies = fetch(source, mortar, sems)
    groups = weights.shape[1] // LANES

    def group(g, lane):
        at = pl.ds(lane, LANES)
        force = jnp.concatenate(adjoint(mortar, lane, weights[:, at]), 0)
        forces[:, at] = jnp.concatenate(cut(force), 0)
        hits[:, at] = indicator(pair[pl.ds(g, 1), :], LANES)

    over_groups(copies, groups, group)
    sums = across(forces[...], hits[...])
    for g, rows in enumerate(merge(face_sums(sums, faces, nodes), 16)):
        out[8 * g : 8 * g + 8, :] = own[8 * g : 8 * g + 8, :] + rows


def face_sums(sums, faces, nodes):
    faces[...] = jnp.zeros(faces.shape, F32)
    faces[0:36, :] = sums[0:36] + sums[80:116]
    faces[36:72, :] = sums[40:76] + sums[120:156]
    return add_faces(faces, nodes)

def last_kernel(arrived, slots, nodes, base, p0, p1, p2, p3, halo, load, residual, applied, tails, forces, hits, faces):
    get_tails(arrived, tails, 32)

    def group(i, carry):
        at = pl.multiple_of(8 * i, 8)
        words = get_words(arrived, pl.multiple_of(40 * i, 8), tails[pl.ds(at, 8), :])
        first, second, _ = decode(words)
        force = jnp.concatenate([first, second], 0)
        lane = pl.multiple_of(LANES * i, LANES)
        forces[:, pl.ds(lane, LANES)] = jnp.concatenate(cut(force), 0)
        hits[:, pl.ds(lane, LANES)] = indicator(slots[pl.ds(i, 1), :], LANES)
        return carry

    lax.fori_loop(0, 32, group, 0, unroll=True)
    total = face_sums(across(forces[...], hits[...]), faces, nodes)
    for o, piece in enumerate((p0, p1, p2, p3)):
        total = total + scatter(piece[...], halo[o : o + 1, :], 16)
    for g, rows in enumerate(merge(total, 16)):
        rows = rows + base[8 * g : 8 * g + 8, :]
        at = WIDE * g
        residual[:, at : at + WIDE] = load[:, at : at + WIDE] - rows[0:3]
        applied[:, at : at + WIDE] = rows[3:6]


def shape(dims, kind=F32):
    return jax.ShapeDtypeStruct(dims, kind)


def settled(*arrays):
    return [pltpu.with_memory_space_constraint(array, pltpu.HBM) for array in arrays]


def call(kernel, results, scratch, flops, size, room, **extra):
    return pl.pallas_call(
        kernel,
        out_shape=results,
        scratch_shapes=scratch,
        compiler_params=pltpu.CompilerParams(vmem_limit_bytes=room * MIB),
        cost_estimate=pl.CostEstimate(flops=flops, bytes_accessed=size, transcendentals=0),
        **extra,
    )


def pack(disp, direction, halo_send, masters, send, count):
    groups = send.shape[1] // 4
    piece = shape((8, halo_send.shape[1]))
    return call(
        pack_kernel,
        [piece] * 4 + [shape((WORDS * send.shape[1], LANES), I32), shape((groups, LANES), I32)],
        [
            pltpu.VMEM((128, WIDE), F32),
            pltpu.VMEM((96, LANES), F32),
            pltpu.VMEM((LANES, LANES), I32),
            pltpu.VMEM((8 * groups, LANES), I32),
        ],
        10**9,
        10**6,
        8,
    )(*settled(disp, direction, halo_send, masters, send, count))


def inputs(count):
    vmem = pl.BlockSpec(memory_space=pltpu.VMEM)
    return [vmem] * count + [pl.BlockSpec(memory_space=pl.ANY)]


def mortar_scratch(mortar, stretches):
    return [pltpu.VMEM(mortar.shape, F32), pltpu.SemaphoreType.DMA((stretches,))]


def near_part(disp, direction, slaves, pair, mortar, gap):
    pairs = mortar.shape[2]
    return call(
        near_kernel,
        shape((24, pairs)),
        [
            pltpu.VMEM((128, WIDE), F32),
            pltpu.VMEM((96, LANES), F32),
            pltpu.VMEM((80, pairs), F32),
        ]
        + mortar_scratch(mortar, 8),
        10**9,
        6 * 10**6,
        14,
        in_specs=inputs(5),
    )(*settled(disp, direction, slaves, pair, gap, mortar))


def elements_part(disp, direction, pieces, nodes, blocks):
    elements = nodes.shape[1]
    return call(
        element_kernel,
        [shape((128, WIDE))] + [shape((8, WIDE))] * 4,
        [
            pltpu.VMEM((160, WIDE), F32),
            pltpu.VMEM((WIDE, 32 * elements), BF16),
            pltpu.VMEM((elements // LANES, 256, LANES), F32),
            pltpu.VMEM((elements // LANES, 256, LANES), F32),
            pltpu.VMEM(blocks.shape, BF16),
            pltpu.VMEM((320, WIDE), F32),
            pltpu.SemaphoreType.DMA((4,)),
        ],
        4 * 10**9,
        10**7,
        32,
        in_specs=inputs(7),
    )(*settled(disp, direction), *pieces, *settled(nodes, blocks))


def far_part(arrived, near, mortar, pieces):
    pairs = mortar.shape[2]
    tails = pltpu.VMEM((8 * (pairs // LANES), LANES), I32)
    return call(
        far_kernel,
        [shape(arrived.shape, I32), shape((24, pairs))],
        [tails, tails] + mortar_scratch(mortar, 4),
        10**9,
        6 * 10**6,
        14,
        in_specs=inputs(6),
    )(arrived, near, pieces[2], pieces[3], pieces[0], pieces[1], *settled(mortar))


def sum_scratch(pairs):
    return [
        pltpu.VMEM((160, pairs), BF16),
        pltpu.VMEM((LANES, pairs), BF16),
        pltpu.VMEM((96, LANES), F32),
    ]


def slave_part(own, slaves, pair, mortar, weights):
    pairs = mortar.shape[2]
    return call(
        slave_kernel,
        shape((128, WIDE)),
        sum_scratch(pairs) + mortar_scratch(mortar, 8),
        10**9,
        6 * 10**6,
        14,
        in_specs=inputs(4),
    )(own, *settled(slaves, pair), weights, *settled(mortar))


def last_part(returned, slots, masters, base, shared, halo_send, load):
    groups = slots.shape[0]
    return call(
        last_kernel,
        [shape(load.shape), shape(load.shape)],
        [pltpu.VMEM((8 * groups, LANES), I32)] + sum_scratch(groups * LANES),
        10**9,
        10**6,
        10,
    )(returned, slots, *settled(masters), base, *shared, *settled(halo_send, load))


def on_device(
    disp,
    direction,
    load,
    blocks,
    elem_nodes,
    halo_send,
    master_nodes,
    slave_nodes,
    mortar_send,
    mortar_count,
    pair_slave,
    slave_mortar,
    master_mortar,
    gap_offset,
):
    peers = lax.axis_size("dom")
    moves = offsets()
    masters, slaves = master_nodes.T, slave_nodes.T
    send = mortar_send[0].T
    pair = pair_slave.reshape(-1, LANES)

    def exchange(value):
        value = value.reshape(peers, 1, WORDS * LANES)
        value = lax.all_to_all(value, "dom", split_axis=0, concat_axis=0, tiled=True)
        return value.reshape(WORDS * peers, LANES)

    packed = pack(disp, direction, halo_send, masters, send, mortar_count)
    outgoing, words, slots = packed[:4], packed[4], packed[5]
    arrived = exchange(words)
    received = {o: shifted(outgoing[o], "dom", moves[o]) for o in (2, 3, 0, 1)}
    pieces = [received[o] for o in range(4)]
    near = near_part(disp, direction, slaves, pair, slave_mortar, gap_offset)
    element = elements_part(disp, direction, pieces, elem_nodes, blocks)
    own, sums = element[0], element[1:]
    shared = [shifted(sums[o], "dom", -moves[o]) for o in range(4)]
    back, weights = far_part(arrived, near, master_mortar, pieces)
    returned = exchange(back)
    base = slave_part(own, slaves, pair, slave_mortar, weights)
    return last_part(returned, slots, masters, base, shared, halo_send, load)


def solution(mesh):
    return jax.shard_map(
        on_device,
        mesh=mesh,
        in_specs=(
            P(None, "dom"),
            P(None, "dom"),
            P(None, "dom"),
            P(None, None, "dom"),
            P(None, "dom"),
            P("dom", None),
            P("dom", None),
            P("dom", None),
            P("dom", None, None),
            P("dom", None),
            P("dom"),
            P(None, None, "dom"),
            P(None, None, "dom"),
            P(None, "dom"),
        ),
        out_specs=(P(None, "dom"), P(None, "dom")),
        check_vma=False,
    )
```

```python
import jax
import jax.numpy as jnp
from jax import lax
from jax.experimental import pallas as pl
from jax.experimental.pallas import tpu as pltpu
from jax.sharding import PartitionSpec as P

REACH = 2
F32, BF16, I32 = jnp.float32, jnp.bfloat16, jnp.int32
LANES = 128
WIDE = 256
WORDS = 10
QUADS = 9
FACE = 12
LIMIT = 32767.0
MIB = 1024 * 1024


def offsets():
    return [move for move in range(-REACH, REACH + 1) if move != 0]


def shifted(value, axis, steps):
    count = lax.axis_size(axis)
    pairs = [(source, (source + steps) % count) for source in range(count)]
    return lax.ppermute(value, axis, pairs)


def indicator(row, count):
    number = lax.broadcasted_iota(jnp.int16, (count, row.shape[1]), 0)
    return jnp.where(number == row.astype(jnp.int16), jnp.ones((), BF16), jnp.zeros((), BF16))


def cut(value):
    high = value.astype(BF16)
    return high, (value - high.astype(F32)).astype(BF16)


def choose(wide, group, groups):
    total = jnp.where(group == 0, wide[0:8], 0.0)
    for g in range(1, groups):
        total = total + jnp.where(group == g, wide[8 * g : 8 * g + 8], 0.0)
    return total


def gather(parts, row, groups):
    hits = indicator(row & (WIDE - 1), WIDE)
    wide = jnp.dot(parts[0], hits, preferred_element_type=F32)
    for part in parts[1:]:
        wide = wide + jnp.dot(part, hits, preferred_element_type=F32)
    return choose(wide, row >> 8, groups)


def place(value, group, groups):
    both = jnp.concatenate(cut(value), 0)
    group = jnp.broadcast_to(group, both.shape).astype(jnp.int16)
    zero = jnp.zeros(both.shape, BF16)
    return jnp.concatenate([jnp.where(group == g, both, zero) for g in range(groups)], 0)


def scatter(value, row, groups):
    wide = place(value, row >> 8, groups)
    hits = indicator(row & (WIDE - 1), WIDE)
    return across(wide, hits)


def across(left, right):
    return lax.dot_general(left, right, (((1,), (1,)), ((), ())), preferred_element_type=F32)


def fill_table(table, disp, direction):
    table[...] = jnp.zeros(table.shape, F32)
    for g in range(disp.shape[1] // WIDE):
        table[8 * g : 8 * g + 3, :] = disp[:, WIDE * g : WIDE * g + WIDE]
        table[8 * g + 3 : 8 * g + 6, :] = direction[:, WIDE * g : WIDE * g + WIDE]


def turn(v):
    lane = lax.broadcasted_iota(I32, v[0].shape, 1)
    low = lane < 64
    even = (lane & 32) == 0
    a0 = jnp.where(low, v[0], pltpu.roll(v[2], 64, 1))
    a2 = jnp.where(low, pltpu.roll(v[0], 64, 1), v[2])
    a1 = jnp.where(low, v[1], pltpu.roll(v[3], 64, 1))
    a3 = jnp.where(low, pltpu.roll(v[1], 64, 1), v[3])
    return [
        jnp.where(even, a0, pltpu.roll(a1, 32, 1)),
        jnp.where(even, pltpu.roll(a0, 96, 1), a1),
        jnp.where(even, a2, pltpu.roll(a3, 32, 1)),
        jnp.where(even, pltpu.roll(a2, 96, 1), a3),
    ]


def put_words(out, base, tails, words):
    for b, block in enumerate(turn([words[8 * q : 8 * q + 8] for q in range(4)])):
        out[pl.ds(base + WORDS * b, 8), :] = block
    tails[...] = words[32:40]


def put_tails(out, tails, count):
    for h in range(2):
        rows = turn([tails[pl.ds(4 * h + q, count, stride=8), :] for q in range(4)])
        for b in range(4):
            out[pl.ds(WORDS * b + 8 + h, count, stride=4 * WORDS), :] = rows[b]


def get_tails(source, tails, count):
    for h in range(2):
        rows = turn(
            [source[pl.ds(WORDS * b + 8 + h, count, stride=4 * WORDS), :] for b in range(4)]
        )
        for q in range(4):
            tails[pl.ds(4 * h + q, count, stride=8), :] = rows[q]


def get_words(source, base, tail):
    blocks = turn([source[pl.ds(base + WORDS * b, 8), :] for b in range(4)])
    return jnp.concatenate(blocks + [tail], 0)


def step_of(level):
    return jnp.exp(level.astype(F32) * (0.25 * 0.6931471805599453))


def level_of(values):
    top = jnp.max(jnp.abs(values), axis=0, keepdims=True)
    return jnp.ceil(jnp.log(jnp.maximum(top, 1e-30)) * (4.0 / 0.6931471805599453))


def split_words(words):
    second = (words << 16) >> 16
    first = (words - second) >> 16
    return first, second


def decode(words):
    out = []
    row = lax.broadcasted_iota(I32, (8, LANES), 0)
    halves = split_words(words)
    for half in halves:
        scale = step_of(half[36:37]) * (1.0 / LIMIT)
        value = half.astype(F32) * scale
        out.append(jnp.concatenate([value[:32], jnp.where(row < 4, value[32:40], 0.0)], 0))
    return out[0], out[1], halves[0][37:38].astype(F32)


def encode(values):
    level = level_of(values)
    code = jnp.round(values * (LIMIT / step_of(level)))
    row = lax.broadcasted_iota(I32, values.shape, 0)
    return jnp.where(row == 36, level, code)


def fold2(a, b, distance):
    row = lax.broadcasted_iota(I32, a.shape, 0)
    first = (row & distance) == 0
    return jnp.where(first, a, b) + pltpu.roll(jnp.where(first, b, a), 8 - distance, 0)


def fold(v):
    v = [fold2(v[2 * r], v[2 * r + 1], 1) for r in range(4)]
    v = [fold2(v[2 * r], v[2 * r + 1], 2) for r in range(2)]
    return fold2(v[0], v[1], 4)


def tail_rows(block):
    return jnp.concatenate([block, jnp.zeros((4, LANES), F32)], 0)


def contract(mortar, lane, first, second):
    sums = ([], [])
    for q in range(QUADS):
        pieces = [mortar[q, 8 * t : 8 * t + 8, pl.ds(lane, LANES)] for t in range(4)]
        pieces.append(tail_rows(mortar[q, 32:36, pl.ds(lane, LANES)]))
        for field, out in zip((first, second), sums):
            total = pieces[0] * field[0:8]
            for t in range(1, 5):
                total = total + pieces[t] * field[8 * t : 8 * t + 8]
            out.append(total)
    last = fold2(sums[0][8], sums[1][8], 1)
    last = last + pltpu.roll(last, 6, 0)
    last = last + pltpu.roll(last, 4, 0)
    return fold(sums[0][:8]), fold(sums[1][:8]), last


def adjoint(mortar, lane, weights):
    rows = [(weights[q : q + 1], weights[8 + q : 9 + q]) for q in range(8)]
    rows.append((weights[16:17], weights[17:18]))
    sums = []
    for t in range(5):
        pair = [None, None]
        for q in range(QUADS):
            if t < 4:
                piece = mortar[q, 8 * t : 8 * t + 8, pl.ds(lane, LANES)]
            else:
                piece = tail_rows(mortar[q, 32:36, pl.ds(lane, LANES)])
            for w in range(2):
                term = piece * rows[q][w]
                pair[w] = term if q == 0 else pair[w] + term
        sums.append(pair)
    return [jnp.concatenate([pair[w] for pair in sums], 0) for w in range(2)]


def fill_faces(faces, parts, nodes):
    for a in range(FACE):
        faces[pl.ds(a, 8, stride=FACE), :] = gather(parts, nodes[a : a + 1, :], 16)


def padded_fields(faces):
    pad = jnp.zeros((4, LANES), F32)
    return jnp.concatenate([faces[0:36], pad], 0), jnp.concatenate([faces[36:72], pad], 0)


def pack_kernel(disp, direction, halo, nodes, send, count, s0, s1, s2, s3, out, slots, table, faces, square, tails):
    fill_table(table, disp, direction)
    parts = cut(table[...])
    for o, piece in enumerate((s0, s1, s2, s3)):
        piece[...] = gather(parts[:1], halo[o : o + 1, :], 16)
    fill_faces(faces, parts, nodes)
    first, second = padded_fields(faces)
    row = lax.broadcasted_iota(I32, first.shape, 0)
    codes = [encode(first), encode(second)]
    codes[0] = jnp.where(row == 37, 1.0, codes[0])
    left = []
    for code in codes:
        high = jnp.floor(code * (1.0 / 256.0))
        left += [high, code - 256.0 * high]
    left = jnp.concatenate(left, 0).astype(BF16)
    square[...] = jnp.zeros(square.shape, I32)
    square[0:32, :] = send[...]
    square[32:33, :] = count[...]
    turned = square[...].T
    lane = lax.broadcasted_iota(I32, turned.shape, 1)
    square[...] = jnp.where(lane < turned[:, 32:33], turned, -1)
    lane = lax.broadcasted_iota(I32, (32, LANES), 1)
    rows = square[pl.ds(0, 32, stride=4), :]
    for b in range(1, 4):
        moved = pltpu.roll(square[pl.ds(b, 32, stride=4), :], 32 * b, 1)
        rows = jnp.where((lane >> 5) == b, moved, rows)
    slots[...] = rows

    def group_pair(i, carry):
        hits = [indicator(slots[pl.ds(2 * i + t, 1), :], LANES) for t in range(2)]
        wide = jnp.dot(left, jnp.concatenate(hits, 1), preferred_element_type=F32)
        for t in range(2):
            here = wide[:, LANES * t : LANES * t + LANES]
            first = (here[0:40] * 256.0 + here[40:80]).astype(I32)
            second = (here[80:120] * 256.0 + here[120:160]).astype(I32)
            base = pl.multiple_of(80 * i, 8) + 40 * t
            at = pl.multiple_of(16 * i, 8) + 8 * t
            put_words(out, base, tails.at[pl.ds(at, 8), :], (first << 16) + second)
        return carry

    lax.fori_loop(0, 16, group_pair, 0, unroll=True)
    put_tails(out, tails, 32)


def element_kernel(fields, p0, p1, p2, p3, nodes, blocks, own, s0, s1, s2, s3, hits, x, y, held, sums, sems):
    chunk = blocks.shape[0] // sems.shape[0]
    copies = [
        pltpu.make_async_copy(
            blocks.at[pl.ds(chunk * n, chunk)], held.at[pl.ds(chunk * n, chunk)], sems.at[n]
        )
        for n in range(sems.shape[0])
    ]
    for copy in copies:
        copy.start()
    pieces = [piece[...] for piece in (p0, p1, p2, p3)]
    coarse = jnp.concatenate([fields[...]] + pieces, 0).astype(BF16)
    elements = nodes.shape[1]

    def gather_node(a, carry):
        for h in range(elements // WIDE):
            row = nodes[pl.ds(a, 1), WIDE * h : WIDE * h + WIDE]
            hit = indicator(row & (WIDE - 1), WIDE)
            at = pl.multiple_of(a * elements, WIDE) + WIDE * h
            hits[:, pl.ds(at, WIDE)] = hit
            wide = jnp.dot(coarse, hit, preferred_element_type=F32)
            picked = choose(wide, row >> 8, 20)
            for part in range(WIDE // LANES):
                x[2 * h + part, pl.ds(a, 8, stride=32), :] = picked[
                    :, LANES * part : LANES * part + LANES
                ]
        return carry

    lax.fori_loop(0, 32, gather_node, 0, unroll=16)
    y[:, 192:256, :] = jnp.zeros((y.shape[0], 64, LANES), F32)
    for n, copy in enumerate(copies):
        copy.wait()
        for part in range(elements // LANES):

            def eight_rows(i, carry, part=part, n=n):
                u, v = [], []
                for r in range(8):
                    block = held[
                        chunk * n + 8 * i + r, :, LANES * part : LANES * part + LANES
                    ].astype(F32)
                    for w, out in enumerate((u, v)):
                        total = block[0:8] * x[part, 96 * w : 96 * w + 8, :]
                        for t in range(1, 12):
                            total = total + block[8 * t : 8 * t + 8] * x[
                                part, 96 * w + 8 * t : 96 * w + 8 * t + 8, :
                            ]
                        out.append(total)
                at = pl.multiple_of(chunk * n + 8 * i, 8)
                y[part, pl.ds(at, 8), :] = fold(u)
                y[part, pl.ds(96 + at, 8), :] = fold(v)
                return carry

            lax.fori_loop(0, chunk // 8, eight_rows, 0, unroll=3)
    sums[...] = jnp.zeros(sums.shape, F32)

    def scatter_node(a, carry):
        for h in range(elements // WIDE):
            row = nodes[pl.ds(a, 1), WIDE * h : WIDE * h + WIDE] >> 8
            value = jnp.concatenate(
                [y[2 * h + part, pl.ds(a, 8, stride=32), :] for part in range(2)], 1
            )
            wide = place(value, row, 20)
            at = pl.multiple_of(a * elements, WIDE) + WIDE * h
            sums[...] += across(wide, hits[:, pl.ds(at, WIDE)])
        return carry

    lax.fori_loop(0, 32, scatter_node, 0, unroll=16)
    for g in range(16):
        own[8 * g : 8 * g + 8, :] = sums[16 * g : 16 * g + 8, :] + sums[16 * g + 8 : 16 * g + 16, :]
    for o, piece in enumerate((s0, s1, s2, s3)):
        g = 16 + o
        piece[...] = sums[16 * g : 16 * g + 8, :] + sums[16 * g + 8 : 16 * g + 16, :]


def fetch(source, held, sems):
    count = sems.shape[0]
    part = source.shape[2] // count
    copies = []
    for n in range(count):
        at = pl.ds(part * n, part)
        copies.append(pltpu.make_async_copy(source.at[:, :, at], held.at[:, :, at], sems.at[n]))
        copies[-1].start()
    return copies


def over_groups(copies, groups, body):
    part = groups // len(copies)
    for n, copy in enumerate(copies):
        copy.wait()

        def step(i, carry, n=n):
            body(part * n + i, pl.multiple_of(LANES * (part * n + i), LANES))
            return carry

        lax.fori_loop(0, part, step, 0, unroll=True)


def near_kernel(table, nodes, pair, gap, source, out, faces, fields, mortar, sems):
    copies = fetch(source, mortar, sems)
    fill_faces(faces, cut(table[...]), nodes)
    left = jnp.concatenate(cut(jnp.concatenate(padded_fields(faces), 0)), 0)
    groups = out.shape[1] // LANES
    for i in range(groups // 2):
        hits = [indicator(pair[2 * i + t : 2 * i + t + 1, :], LANES) for t in range(2)]
        wide = jnp.dot(left, jnp.concatenate(hits, 1), preferred_element_type=F32)
        fields[:, 2 * LANES * i : 2 * LANES * (i + 1)] = wide[:80] + wide[80:]
    number = lax.broadcasted_iota(I32, (8, LANES), 0)

    def group(g, lane):
        at = pl.ds(lane, LANES)
        opening, tangent, last = contract(mortar, lane, fields.at[0:40, at], fields.at[40:80, at])
        out[0:8, at] = opening + gap[0:8, at]
        out[8:16, at] = tangent
        out[16:24, at] = last + jnp.where((number & 1) == 0, gap[8:9, at], 0.0)

    over_groups(copies, groups, group)

def react(opening, tangent, live):
    fade = jnp.exp(-jnp.abs(opening))
    pressure = jnp.maximum(opening, 0.0) + jnp.log1p(fade)
    share = jnp.where(opening >= 0.0, 1.0, fade) / (1.0 + fade)
    return pressure * live, share * tangent * live


def far_kernel(arrived, near, p0, p1, p2, p3, source, out, weights, tails, back, mortar, sems):
    copies = fetch(source, mortar, sems)
    groups = near.shape[1] // LANES
    get_tails(arrived, tails, groups)
    number = lax.broadcasted_iota(I32, (8, LANES), 0)

    def group(g, lane):
        at = pl.ds(lane, LANES)
        base = pl.multiple_of(40 * g, 8)
        eight = pl.ds(pl.multiple_of(8 * g, 8), 8)
        first, second, live = decode(get_words(arrived, base, tails[eight, :]))
        opening, tangent, last = contract(mortar, lane, first, second)
        opening = opening + near[0:8, at]
        tangent = tangent + near[8:16, at]
        last = last + near[16:24, at]
        pressure, increment = react(opening, tangent, live)
        ninth = react(last[0:1], last[1:2], live)
        ninth = jnp.where((number & 1) == 0, ninth[0], ninth[1])
        here = jnp.concatenate([pressure, increment, ninth], 0)
        weights[:, at] = here
        first, second = (encode(force).astype(I32) for force in adjoint(mortar, lane, here))
        put_words(out, base, back.at[eight, :], (first << 16) + second)

    over_groups(copies, groups, group)
    put_tails(out, back, groups)

def add_faces(faces, nodes):
    total = None
    for a in range(FACE):
        term = scatter(faces[pl.ds(a, 8, stride=FACE), :], nodes[a : a + 1, :], 16)
        total = term if a == 0 else total + term
    return total


def merge(total, groups):
    return [total[16 * g : 16 * g + 8] + total[16 * g + 8 : 16 * g + 16] for g in range(groups)]


def slave_kernel(own, nodes, pair, weights, source, out, forces, hits, faces, mortar, sems):
    copies = fetch(source, mortar, sems)
    groups = weights.shape[1] // LANES

    def group(g, lane):
        at = pl.ds(lane, LANES)
        force = jnp.concatenate(adjoint(mortar, lane, weights[:, at]), 0)
        forces[:, at] = jnp.concatenate(cut(force), 0)

    for g in range(groups):
        hits[:, LANES * g : LANES * g + LANES] = indicator(pair[g : g + 1, :], LANES)
    over_groups(copies, groups, group)
    sums = across(forces[...], hits[...])
    for g, rows in enumerate(merge(face_sums(sums, faces, nodes), 16)):
        out[8 * g : 8 * g + 8, :] = own[8 * g : 8 * g + 8, :] + rows


def face_sums(sums, faces, nodes):
    faces[...] = jnp.zeros(faces.shape, F32)
    faces[0:36, :] = sums[0:36] + sums[80:116]
    faces[36:72, :] = sums[40:76] + sums[120:156]
    return add_faces(faces, nodes)

def last_kernel(arrived, slots, nodes, base, p0, p1, p2, p3, halo, load, residual, applied, tails, forces, hits, faces):
    get_tails(arrived, tails, 32)

    def group(i, carry):
        at = pl.multiple_of(8 * i, 8)
        words = get_words(arrived, pl.multiple_of(40 * i, 8), tails[pl.ds(at, 8), :])
        first, second, _ = decode(words)
        force = jnp.concatenate([first, second], 0)
        lane = pl.multiple_of(LANES * i, LANES)
        forces[:, pl.ds(lane, LANES)] = jnp.concatenate(cut(force), 0)
        hits[:, pl.ds(lane, LANES)] = indicator(slots[pl.ds(i, 1), :], LANES)
        return carry

    lax.fori_loop(0, 32, group, 0, unroll=True)
    total = face_sums(across(forces[...], hits[...]), faces, nodes)
    for o, piece in enumerate((p0, p1, p2, p3)):
        total = total + scatter(piece[...], halo[o : o + 1, :], 16)
    for g, rows in enumerate(merge(total, 16)):
        rows = rows + base[8 * g : 8 * g + 8, :]
        at = WIDE * g
        residual[:, at : at + WIDE] = load[:, at : at + WIDE] - rows[0:3]
        applied[:, at : at + WIDE] = rows[3:6]


def shape(dims, kind=F32):
    return jax.ShapeDtypeStruct(dims, kind)


def settled(*arrays):
    return [pltpu.with_memory_space_constraint(array, pltpu.HBM) for array in arrays]


def call(kernel, results, scratch, flops, size, room, **extra):
    return pl.pallas_call(
        kernel,
        out_shape=results,
        scratch_shapes=scratch,
        compiler_params=pltpu.CompilerParams(vmem_limit_bytes=room * MIB),
        cost_estimate=pl.CostEstimate(flops=flops, bytes_accessed=size, transcendentals=0),
        **extra,
    )


def pack(disp, direction, halo_send, masters, send, count):
    groups = send.shape[1] // 4
    piece = shape((8, halo_send.shape[1]))
    return call(
        pack_kernel,
        [piece] * 4
        + [
            shape((WORDS * send.shape[1], LANES), I32),
            shape((groups, LANES), I32),
            shape((128, WIDE)),
        ],
        [
            pltpu.VMEM((96, LANES), F32),
            pltpu.VMEM((LANES, LANES), I32),
            pltpu.VMEM((8 * groups, LANES), I32),
        ],
        10**9,
        10**6,
        8,
    )(*settled(disp, direction, halo_send, masters, send, count))


def inputs(count):
    vmem = pl.BlockSpec(memory_space=pltpu.VMEM)
    return [vmem] * count + [pl.BlockSpec(memory_space=pl.ANY)]


def mortar_scratch(mortar, stretches):
    return [pltpu.VMEM(mortar.shape, F32), pltpu.SemaphoreType.DMA((stretches,))]


def near_part(table, slaves, pair, mortar, gap):
    pairs = mortar.shape[2]
    return call(
        near_kernel,
        shape((24, pairs)),
        [pltpu.VMEM((96, LANES), F32), pltpu.VMEM((80, pairs), F32)]
        + mortar_scratch(mortar, 8),
        10**9,
        6 * 10**6,
        14,
        in_specs=inputs(4),
    )(table, *settled(slaves, pair, gap, mortar))


def elements_part(table, pieces, nodes, blocks):
    elements = nodes.shape[1]
    return call(
        element_kernel,
        [shape((128, WIDE))] + [shape((8, WIDE))] * 4,
        [
            pltpu.VMEM((WIDE, 32 * elements), BF16),
            pltpu.VMEM((elements // LANES, 256, LANES), F32),
            pltpu.VMEM((elements // LANES, 256, LANES), F32),
            pltpu.VMEM(blocks.shape, BF16),
            pltpu.VMEM((320, WIDE), F32),
            pltpu.SemaphoreType.DMA((4,)),
        ],
        4 * 10**9,
        10**7,
        32,
        in_specs=inputs(6),
    )(table, *pieces, *settled(nodes, blocks))


def far_part(arrived, near, mortar, pieces):
    pairs = mortar.shape[2]
    tails = pltpu.VMEM((8 * (pairs // LANES), LANES), I32)
    return call(
        far_kernel,
        [shape(arrived.shape, I32), shape((24, pairs))],
        [tails, tails] + mortar_scratch(mortar, 4),
        10**9,
        6 * 10**6,
        14,
        in_specs=inputs(6),
    )(arrived, near, pieces[2], pieces[3], pieces[0], pieces[1], *settled(mortar))


def sum_scratch(pairs):
    return [
        pltpu.VMEM((160, pairs), BF16),
        pltpu.VMEM((LANES, pairs), BF16),
        pltpu.VMEM((96, LANES), F32),
    ]


def slave_part(own, slaves, pair, mortar, weights):
    pairs = mortar.shape[2]
    return call(
        slave_kernel,
        shape((128, WIDE)),
        sum_scratch(pairs) + mortar_scratch(mortar, 8),
        10**9,
        6 * 10**6,
        14,
        in_specs=inputs(4),
    )(own, *settled(slaves, pair), weights, *settled(mortar))


def last_part(returned, slots, masters, base, shared, halo_send, load):
    groups = slots.shape[0]
    return call(
        last_kernel,
        [shape(load.shape), shape(load.shape)],
        [pltpu.VMEM((8 * groups, LANES), I32)] + sum_scratch(groups * LANES),
        10**9,
        10**6,
        10,
    )(returned, slots, *settled(masters), base, *shared, *settled(halo_send, load))


def on_device(
    disp,
    direction,
    load,
    blocks,
    elem_nodes,
    halo_send,
    master_nodes,
    slave_nodes,
    mortar_send,
    mortar_count,
    pair_slave,
    slave_mortar,
    master_mortar,
    gap_offset,
):
    peers = lax.axis_size("dom")
    moves = offsets()
    masters, slaves = master_nodes.T, slave_nodes.T
    send = mortar_send[0].T
    pair = pair_slave.reshape(-1, LANES)

    def exchange(value):
        value = value.reshape(peers, 1, WORDS * LANES)
        value = lax.all_to_all(value, "dom", split_axis=0, concat_axis=0, tiled=True)
        return value.reshape(WORDS * peers, LANES)

    packed = pack(disp, direction, halo_send, masters, send, mortar_count)
    outgoing, words, slots, table = packed[:4], packed[4], packed[5], packed[6]
    arrived = exchange(words)
    received = {o: shifted(outgoing[o], "dom", moves[o]) for o in (2, 3, 0, 1)}
    pieces = [received[o] for o in range(4)]
    near = near_part(table, slaves, pair, slave_mortar, gap_offset)
    element = elements_part(table, pieces, elem_nodes, blocks)
    own, sums = element[0], element[1:]
    shared = [shifted(sums[o], "dom", -moves[o]) for o in range(4)]
    back, weights = far_part(arrived, near, master_mortar, pieces)
    returned = exchange(back)
    base = slave_part(own, slaves, pair, slave_mortar, weights)
    return last_part(returned, slots, masters, base, shared, halo_send, load)


def solution(mesh):
    return jax.shard_map(
        on_device,
        mesh=mesh,
        in_specs=(
            P(None, "dom"),
            P(None, "dom"),
            P(None, "dom"),
            P(None, None, "dom"),
            P(None, "dom"),
            P("dom", None),
            P("dom", None),
            P("dom", None),
            P("dom", None, None),
            P("dom", None),
            P("dom"),
            P(None, None, "dom"),
            P(None, None, "dom"),
            P(None, "dom"),
        ),
        out_specs=(P(None, "dom"), P(None, "dom")),
        check_vma=False,
    )
```
